32 devices in a mesh: dp: 8 (over z, y), tensor: 4 (over x, core).
Axes of the slice: x: 2, y: 2, z: 4, core: 2. Of those that a mesh axis runs over, the one named last changes fastest.
Arguments:
- inputs: bfloat16 [4096, 4096], P('dp'), may hold values from -6 to 6
- weight: bfloat16 [4096, 4096], P(None, 'tensor'), may hold values from -0.09375 to 0.09375
- targets: bfloat16 [4096, 4096], P('dp', 'tensor'), may hold values from -6 to 6
- momentum: float32 [4096, 4096], P('dp', 'tensor'), may hold values from -6 to 6
Outputs:
- input_grad: bfloat16 [4096, 4096], P('tensor', 'dp')
- new_momentum: float32 [4096, 4096], P('dp', 'tensor')
- tree_norms: float32 [2], replicated
The draws below stay inside these ranges and needn't reach their ends.
All inputs are finite; a program needn't handle non-finite values.
Results may differ from the reference program's by a relative error of at most 0.013.
Values may be sent and summed in bfloat16 or wider, within the bound.
No kernel may reach another device: no remote copies, remote signals or barrier semaphores. Data moves between devices by JAX's collectives and lax.ppermute only.
A program may use at most 128 MiB of HBM per device.

```python
import math
import jax
import jax.numpy as jnp
from jax import lax

D = 4096
ROWS = 512
TOTAL_ROWS = 4096
N_DP = 8
N_TENSOR = 4


def block_levels(stream_key, shape, cuts, least, top_value):
    factor_of, own = 1.0, jax.random.fold_in(stream_key, 6)
    for axis_at, blocks in cuts:
        steps = jnp.exp(jax.random.uniform(jax.random.fold_in(own, axis_at), (blocks,), jnp.float32, least / len(cuts), top_value / len(cuts)))
        factor_of = factor_of * jnp.repeat(steps, shape[axis_at] // blocks).reshape([-1 if axis == axis_at else 1 for axis in range(len(shape))])
    return factor_of


def normal_values(key, extent, scale, bound, cuts=(), dtype=jnp.bfloat16):
    gain = block_levels(key, extent, cuts, -0.22, 0.18) if cuts else 1.0
    result = jax.random.normal(key, extent, jnp.float32) * scale * gain
    return jnp.minimum(jnp.maximum(result, -bound), bound).astype(dtype)


def setup_inputs(seed: int = 0) -> dict:
    arg_keys = jax.random.split(jax.random.key(seed), 5)
    inputs = normal_values(arg_keys[0], (TOTAL_ROWS, D), 1.0, 6.0, ((0, 8),))
    weight = normal_values(arg_keys[1], (D, D), D ** -0.5, 0.09375, ((1, 4),))
    targets = normal_values(arg_keys[2], (TOTAL_ROWS, D), 1.0, 6.0, ((0, 8), (1, 4)))
    momentum = normal_values(arg_keys[3], (D, D), 1.0, 6.0, ((0, 8), (1, 4)), jnp.float32)
    return dict(inputs=inputs, weight=weight, targets=targets, momentum=momentum)


def group_terms(inputs_g, targets_g, weight):
    outputs = jnp.dot(inputs_g, weight, preferred_element_type=jnp.float32)
    error = (outputs - targets_g.astype(jnp.float32)).astype(jnp.bfloat16)
    grad = lax.dot_general(inputs_g, error, (((0,), (0,)), ((), ())), preferred_element_type=jnp.float32)
    grad = grad * (1.0 / math.sqrt(ROWS))
    width = D // N_TENSOR
    total = jnp.zeros((D, inputs_g.shape[0]), jnp.float32)
    for block in range(N_TENSOR):
        part = lax.dot_general(weight[:, block * width:(block + 1) * width], error[:, block * width:(block + 1) * width], (((1,), (1,)), ((), ())), preferred_element_type=jnp.float32)
        total = total + part.astype(jnp.bfloat16).astype(jnp.float32)
    return (grad, total.astype(jnp.bfloat16))

def adasum_norms(first, second):
    cross = jnp.sum(first * second)
    first_sq = jnp.sum(first * first)
    second_sq = jnp.sum(second * second)
    merged = (1.0 - cross / (2.0 * first_sq)) * first + (1.0 - cross / (2.0 * second_sq)) * second
    return (merged, first_sq, second_sq)

def reference(inputs, weight, targets, momentum):
    pieces = []

    def combine(lower, count):
        if count == 1:
            grad, partial_grad = group_terms(inputs[lower * ROWS:(lower + 1) * ROWS], targets[lower * ROWS:(lower + 1) * ROWS], weight)
            pieces.append((lower, partial_grad))
            return grad
        half = count // 2
        first = combine(lower, half)
        second = combine(lower + half, half)
        return adasum_norms(first, second)[0]
    half_all = N_DP // 2
    first_all = combine(0, half_all)
    second_all = combine(half_all, half_all)
    combined, first_sq, second_sq = adasum_norms(first_all, second_all)
    ordered = sorted(pieces, key=lambda item: item[0])
    input_grad = jnp.concatenate([item[1] for item in ordered], axis=1)
    tree_norms = jnp.sqrt(jnp.stack([first_sq, second_sq])) / D
    return (input_grad, 0.9 * momentum + combined, tree_norms)
```

```python
import functools
import math

import jax
import jax.numpy as jnp
from jax import lax
from jax.experimental import pallas as pl
from jax.experimental.pallas import tpu as pltpu
from jax.sharding import PartitionSpec as P

QUAD = 4
PAIRS = [(a, b) for a in range(QUAD) for b in range(a, QUAD)]
LANES = 128
VMEM_LIMIT = 40 * 2**20


def exchange(value, axis, mask):
    pairs = [(source, source ^ mask) for source in range(lax.axis_size(axis))]
    return lax.ppermute(value, axis, pairs)


def total_over(value, dp_bits):
    mask = 1
    while mask < lax.axis_size("tensor"):
        value = value + exchange(value, "tensor", mask)
        mask *= 2
    for bit in range(dp_bits):
        value = value + exchange(value, "dp", 2**bit)
    return value


def dot(a, b):
    return jnp.dot(a, b, preferred_element_type=jnp.float32)


def group_products(xt, others, errors):
    e0, e1, e2, e3_top, e3_low = errors
    half = e3_top.shape[0]
    return [
        dot(xt[...], e0[...]),
        dot(others[0, 0], e1[...]),
        dot(others[0, 1], e2[...]),
        dot(others[0, 2, :, :half], e3_top[...]) + dot(others[0, 2, :, half:], e3_low[...]),
    ]


def gram_kernel(idx, xt, others, e0, e1, e2, e3_top, e3_low, out, tiles, acc):
    step = pl.program_id(0)

    @pl.when(step == 0)
    def _():
        acc[...] = jnp.zeros_like(acc)

    for k, tile in enumerate(group_products(xt, others, (e0, e1, e2, e3_top, e3_low))):
        tiles[k] = tile
    rows, columns = tiles.shape[1:]
    chunks = columns // LANES

    def strip(i, sums):
        at = pl.ds(pl.multiple_of(i * 8, 8), 8)
        sums = list(sums)
        for c in range(chunks):
            parts = [tiles[k, at, c * LANES:(c + 1) * LANES] for k in range(QUAD)]
            for n, (a, b) in enumerate(PAIRS):
                sums[n] = sums[n] + parts[a] * parts[b]
        return tuple(sums)

    sums = lax.fori_loop(0, rows // 8, strip, tuple(acc[n] for n in range(len(PAIRS))))
    for n in range(len(PAIRS)):
        acc[n] = sums[n]

    @pl.when(step == pl.num_programs(0) - 1)
    def _():
        lane = lax.broadcasted_iota(jnp.int32, (1, LANES), 1)
        turn = idx[0] * (QUAD + 1)
        result = jnp.zeros((1, LANES), jnp.float32)
        for n, (a, b) in enumerate(PAIRS):
            value = jnp.sum(jnp.sum(acc[n], axis=0, keepdims=True), axis=1, keepdims=True)
            place = jnp.bitwise_xor(QUAD * a + b, turn)
            mirror = jnp.bitwise_xor(QUAD * b + a, turn)
            result = jnp.where((lane == place) | (lane == mirror), value, result)
        out[...] = result


def gram(idx, xt, others, errors):
    steps, _, width, rows = others.shape
    columns = errors[0].shape[1]
    whole = lambda e: pl.BlockSpec(e.shape, lambda j, idx: (0, 0))
    return pl.pallas_call(
        gram_kernel,
        grid_spec=pltpu.PrefetchScalarGridSpec(
            num_scalar_prefetch=1,
            grid=(steps,),
            in_specs=[
                pl.BlockSpec((width, rows), lambda j, idx: (j, 0)),
                pl.BlockSpec((1, QUAD - 1, width, rows), lambda j, idx: (idx[1 + j], 0, 0, 0)),
                *[whole(e) for e in errors],
            ],
            out_specs=pl.BlockSpec((1, LANES), lambda j, idx: (0, 0)),
            scratch_shapes=[
                pltpu.VMEM((QUAD, width, columns), jnp.float32),
                pltpu.VMEM((len(PAIRS), 8, LANES), jnp.float32),
            ],
        ),
        out_shape=jax.ShapeDtypeStruct((1, LANES), jnp.float32),
        compiler_params=pltpu.CompilerParams(vmem_limit_bytes=VMEM_LIMIT),
        cost_estimate=pl.CostEstimate(
            flops=2 * QUAD * steps * width * rows * columns, bytes_accessed=6 * 2**20, transcendentals=0
        ),
        name="gram",
    )(idx, xt, others, *errors)


def merge_factors(gram_at):
    factors = [None] * QUAD
    for a, b in ((0, 1), (2, 3)):
        cross = gram_at(a, b)
        factors[a] = 1.0 - cross / (2.0 * gram_at(a, a))
        factors[b] = 1.0 - cross / (2.0 * gram_at(b, b))

    def product(left, right):
        return sum(factors[a] * factors[b] * gram_at(a, b) for a in left for b in right)

    cross = product((0, 1), (2, 3))
    first = 1.0 - cross / (2.0 * product((0, 1), (0, 1)))
    second = 1.0 - cross / (2.0 * product((2, 3), (2, 3)))
    return [factors[0] * first, factors[1] * first, factors[2] * second, factors[3] * second]


def merge_kernel(scale, idx, gram_ref, xt, others, e0, e1, e2, e3_top, e3_low, out):
    turn = idx[0] * (QUAD + 1)
    factors = merge_factors(lambda a, b: gram_ref[jnp.bitwise_xor(QUAD * a + b, turn)])
    tiles = group_products(xt, others, (e0, e1, e2, e3_top, e3_low))
    total = (factors[0] * scale) * tiles[0]
    for k in range(1, QUAD):
        total = total + (factors[k] * scale) * tiles[k]
    out[...] = total.astype(out.dtype)


def merge(idx, sums, xt, others, errors, dtype):
    _, _, width, rows = others.shape
    steps = (idx.shape[0] - 1) // 2
    columns = errors[0].shape[1]
    whole = lambda e: pl.BlockSpec(e.shape, lambda j, idx, sums: (0, 0))
    return pl.pallas_call(
        functools.partial(merge_kernel, 1.0 / math.sqrt(rows)),
        grid_spec=pltpu.PrefetchScalarGridSpec(
            num_scalar_prefetch=2,
            grid=(steps,),
            in_specs=[
                pl.BlockSpec((width, rows), lambda j, idx, sums: (idx[1 + j], 0)),
                pl.BlockSpec(
                    (1, QUAD - 1, width, rows), lambda j, idx, sums: (idx[1 + steps + j], 0, 0, 0)
                ),
                *[whole(e) for e in errors],
            ],
            out_specs=pl.BlockSpec((width, columns), lambda j, idx, sums: (j, 0)),
        ),
        out_shape=jax.ShapeDtypeStruct((steps * width, columns), dtype),
        compiler_params=pltpu.CompilerParams(vmem_limit_bytes=VMEM_LIMIT),
        cost_estimate=pl.CostEstimate(
            flops=2 * QUAD * steps * width * rows * columns, bytes_accessed=4 * 2**20, transcendentals=0
        ),
        name="merge",
    )(idx, sums.reshape(LANES), xt, others, *errors)


def body(inputs, weight, targets, momentum):
    groups = lax.axis_size("dp")
    parts = lax.axis_size("tensor")
    depth = groups.bit_length() - 1
    me = lax.axis_index("dp")
    part = lax.axis_index("tensor")
    rows, depth_width = inputs.shape
    columns = weight.shape[1]
    block = depth_width // groups
    blocks = groups // QUAD
    width = blocks * block // parts
    per_block = block // width
    place = me % QUAD

    def columns_of(at, start, size):
        first = (QUAD * (start // block) + at) * block + start % block
        return lax.dynamic_slice(inputs, (0, first), (rows, size)).T

    slabs = [exchange(columns_of(place ^ k, part * width, width), "dp", k) for k in range(1, QUAD)]
    others = jnp.stack(slabs)[None]
    mask = parts // 2
    while mask:
        others = jnp.concatenate([others, exchange(others, "tensor", mask)])
        mask //= 2
    own = jnp.concatenate([columns_of(place, b * block, block) for b in range(blocks)])

    def slot(j):
        mask, result, bit = parts // 2, 0, 0
        source = j ^ part
        while mask:
            result = result + ((source & mask) // mask << bit)
            mask, bit = mask // 2, bit + 1
        return result

    halves = []
    for h in range(2):
        at = slice(h * columns // 2, (h + 1) * columns // 2)
        outputs = dot(inputs, weight[:, at])
        halves.append((outputs - targets[:, at].astype(jnp.float32)).astype(jnp.bfloat16))
    errors = []
    for e0 in halves:
        e1 = exchange(e0, "dp", 1)
        e2 = exchange(e0, "dp", 2)
        top = exchange(e2[: rows // 2], "dp", 1)
        low = exchange(e1[rows // 2:], "dp", 2)
        errors.append((e0, e1, e2, top, low))

    idx = jnp.stack([place] + [slot(j) for j in range(parts)]).astype(jnp.int32)
    sums = gram(idx, own, others, errors[0]) + gram(idx, own, others, errors[1])
    sums = total_over(sums, 2)

    error = jnp.concatenate(halves, axis=1)
    summed = lax.psum_scatter(
        lax.dot_general(
            weight, error, (((1,), (1,)), ((), ())), preferred_element_type=jnp.float32
        ).astype(jnp.bfloat16),
        "tensor",
        scatter_dimension=0,
        tiled=True,
    )

    def tiles_of(bit):
        order = [(2 * i + bit) * per_block + s for i in range(blocks // 2) for s in range(per_block)]
        return jnp.stack([place] + order + [slot(j) for j in order]).astype(jnp.int32)

    bit = me >> 2 & 1
    sent = [merge(tiles_of(1 - bit), sums, own, others, e, jnp.bfloat16) for e in errors]
    received = [exchange(s, "dp", 4) for s in sent]
    kept = [merge(tiles_of(bit), sums, own, others, e, jnp.float32) for e in errors]
    for level in range(2, depth):
        if level > 2:
            bit = me >> level & 1
            paired = [v.reshape(v.shape[0] // (2 * block), 2, block, v.shape[1]) for v in merged]
            kept = [jnp.where(bit == 0, v[:, 0], v[:, 1]).reshape(-1, v.shape[-1]) for v in paired]
            sent = [jnp.where(bit == 0, v[:, 1], v[:, 0]).reshape(-1, v.shape[-1]) for v in paired]
            received = [exchange(s.astype(jnp.bfloat16), "dp", 2**level) for s in sent]
        lower = bit == 0
        cross = sum(jnp.sum(a * b.astype(jnp.float32)) for a, b in zip(kept, received))
        mine = sum(jnp.sum(a * a) for a in kept)
        theirs = sum(jnp.sum(jnp.square(b.astype(jnp.float32))) for b in received)
        sums = total_over(
            jnp.stack([cross, jnp.where(lower, mine, theirs), jnp.where(lower, theirs, mine)]), level + 1
        )
        lower_factor = 1.0 - sums[0] / (2.0 * sums[1])
        upper_factor = 1.0 - sums[0] / (2.0 * sums[2])
        factor = jnp.where(lower, lower_factor, upper_factor)
        other = jnp.where(lower, upper_factor, lower_factor)
        merged = [factor * a + other * b.astype(jnp.float32) for a, b in zip(kept, received)]
    combined = jnp.concatenate(merged, axis=1)
    return (summed, 0.9 * momentum + combined, jnp.sqrt(sums[1:3]) / depth_width)


def solution(mesh):
    return jax.shard_map(
        body,
        mesh=mesh,
        in_specs=(P("dp", None), P(None, "tensor"), P("dp", "tensor"), P("dp", "tensor")),
        out_specs=(P("tensor", "dp"), P("dp", "tensor"), P()),
        check_vma=False,
    )
```

```python
import functools
import math

import jax
import jax.numpy as jnp
from jax import lax
from jax.experimental import pallas as pl
from jax.experimental.pallas import tpu as pltpu
from jax.sharding import PartitionSpec as P

QUAD = 4
LANES = 128
VMEM_LIMIT = 18 * 2**20
FULL_VMEM = 60 * 2**20


def exchange(value, axis, mask):
    pairs = [(source, source ^ mask) for source in range(lax.axis_size(axis))]
    return lax.ppermute(value, axis, pairs)


def total_over(value, dp_bits):
    mask = 1
    while mask < lax.axis_size("tensor"):
        value = value + exchange(value, "tensor", mask)
        mask *= 2
    for bit in range(dp_bits):
        value = value + exchange(value, "dp", 2**bit)
    return value


def dot(a, b):
    return jnp.dot(a, b, preferred_element_type=jnp.float32)


def pair_sums(step, pairs, strips, rows, load, acc):
    @pl.when(step == 0)
    def _():
        acc[...] = jnp.zeros_like(acc)

    def strip(i, sums):
        at = pl.ds(pl.multiple_of(i * rows, rows), rows)
        sums = list(sums)
        for tile in load(at):
            for n, (a, b) in enumerate(pairs):
                sums[n] = sums[n] + tile[a] * tile[b]
        return tuple(sums)

    sums = lax.fori_loop(0, strips, strip, tuple(acc[n] for n in range(len(pairs))))
    for n in range(len(pairs)):
        acc[n] = sums[n]


def place_sums(place, pairs, acc, result):
    lane = lax.broadcasted_iota(jnp.int32, (1, LANES), 1)
    turn = place * (QUAD + 1)
    for n, (a, b) in enumerate(pairs):
        value = jnp.sum(jnp.sum(acc[n], axis=0, keepdims=True), axis=1, keepdims=True)
        first = jnp.bitwise_xor(QUAD * a + b, turn)
        second = jnp.bitwise_xor(QUAD * b + a, turn)
        result = jnp.where((lane == first) | (lane == second), value, result)
    return result


def lanes_of(columns):
    return [slice(c, c + LANES) for c in range(0, columns, LANES)]


NEAR_PAIRS = [(a, b) for a in range(QUAD - 1) for b in range(a, QUAD - 1)]
FAR_PAIRS = [(a, QUAD - 1) for a in range(QUAD)]


def forward_kernel(x, w, targets, top, low):
    error = (dot(x[...], w[...]) - targets[...].astype(jnp.float32)).astype(top.dtype)
    half = top.shape[0]
    top[...] = error[:half]
    low[...] = error[half:]


def forward(inputs, weight, targets):
    rows, inner = inputs.shape
    columns = weight.shape[1]
    tile = math.gcd(columns, 256)
    half = jax.ShapeDtypeStruct((rows // 2, columns), jnp.bfloat16)
    return pl.pallas_call(
        forward_kernel,
        grid=(columns // tile,),
        in_specs=[
            pl.BlockSpec((rows, inner), lambda j: (0, 0), pipeline_mode=pl.Buffered(1)),
            pl.BlockSpec((inner, tile), lambda j: (0, j)),
            pl.BlockSpec((rows, tile), lambda j: (0, j)),
        ],
        out_specs=[pl.BlockSpec((rows // 2, tile), lambda j: (0, j))] * 2,
        out_shape=[half, half],
        compiler_params=pltpu.CompilerParams(vmem_limit_bytes=FULL_VMEM),
        cost_estimate=pl.CostEstimate(
            flops=2 * rows * inner * columns, bytes_accessed=14 * 2**20, transcendentals=0
        ),
        name="forward",
    )(inputs, weight, targets)


def input_grad_kernel(w, top, low, out):
    half = top.shape[0]
    for at, error in ((0, top), (half, low)):
        out[:, at:at + half] = lax.dot_general(
            w[...], error[...], (((1,), (1,)), ((), ())), preferred_element_type=jnp.float32
        ).astype(out.dtype)


def input_grad_part(weight, top, low):
    inner, columns = weight.shape
    half = top.shape[0]
    tile = math.gcd(inner, 512)
    whole = pl.BlockSpec((half, columns), lambda j: (0, 0), pipeline_mode=pl.Buffered(1))
    return pl.pallas_call(
        input_grad_kernel,
        grid=(inner // tile,),
        in_specs=[pl.BlockSpec((tile, columns), lambda j: (j, 0)), whole, whole],
        out_specs=pl.BlockSpec((tile, 2 * half), lambda j: (j, 0)),
        out_shape=jax.ShapeDtypeStruct((inner, 2 * half), jnp.bfloat16),
        compiler_params=pltpu.CompilerParams(vmem_limit_bytes=VMEM_LIMIT),
        cost_estimate=pl.CostEstimate(
            flops=4 * inner * half * columns, bytes_accessed=14 * 2**20, transcendentals=0
        ),
        name="input_grad_part",
    )(weight, top, low)


def halves_dot(xt, top, low):
    half = top.shape[0]
    return dot(xt[:, :half], top[...]) + dot(xt[:, half:], low[...])


def near_kernel(pieces, idx, xt, own_top, own_low, y_top, y_low, z_top, z_low, *refs):
    others, (out, grads, tiles, acc) = refs[:pieces], refs[pieces:]
    step = pl.program_id(0)
    tiles[0] = halves_dot(xt, own_top, own_low)
    for q, other in enumerate(others):

        @pl.when(step == q)
        def _():
            tiles[1] = halves_dot(other.at[0], y_top, y_low)
            tiles[2] = halves_dot(other.at[1], z_top, z_low)

    def load(at):
        for lanes in lanes_of(tiles.shape[2]):
            tile = [tiles[k, at, lanes] for k in range(QUAD - 1)]
            for k in range(QUAD - 1):
                grads[k, at, lanes] = tile[k].astype(grads.dtype)
            yield tile

    pair_sums(step, NEAR_PAIRS, tiles.shape[1] // 16, 16, load, acc)

    @pl.when(step == pl.num_programs(0) - 1)
    def _():
        out[...] = place_sums(idx[0], NEAR_PAIRS, acc, jnp.zeros((1, LANES), jnp.float32))


def far_kernel(pieces, idx, before, top, low, grads, *refs):
    others, (out, last, tile, acc) = refs[:pieces], refs[pieces:]
    step = pl.program_id(0)
    for q, other in enumerate(others):

        @pl.when(step == q)
        def _():
            tile[...] = halves_dot(other.at[0], top, low)

    def load(at):
        for lanes in lanes_of(tile.shape[1]):
            mine = tile[at, lanes]
            last[at, lanes] = mine.astype(last.dtype)
            yield [grads[k, at, lanes].astype(jnp.float32) for k in range(QUAD - 1)] + [mine]

    pair_sums(step, FAR_PAIRS, tile.shape[0] // 16, 16, load, acc)

    @pl.when(step == pl.num_programs(0) - 1)
    def _():
        out[...] = place_sums(idx[0], FAR_PAIRS, acc, before[...])


def once(shape, at):
    return pl.BlockSpec(shape, lambda j, idx: at, pipeline_mode=pl.Buffered(1))


PLACE, BIT, TILE = 0, 1, 2


def near_gram(idx, xt, others, errors):
    _, width, rows = others[0].shape
    columns = errors[0].shape[1]
    steps = len(others)
    return pl.pallas_call(
        functools.partial(near_kernel, steps),
        grid_spec=pltpu.PrefetchScalarGridSpec(
            num_scalar_prefetch=1,
            grid=(steps,),
            in_specs=[pl.BlockSpec((width, rows), lambda j, idx: (idx[TILE + j], 0))]
            + [once(e.shape, (0, 0)) for e in errors]
            + [once((QUAD - 2, width, rows), (0, 0, 0))] * steps,
            out_specs=[
                pl.BlockSpec((1, LANES), lambda j, idx: (0, 0)),
                pl.BlockSpec((QUAD - 1, width, columns), lambda j, idx: (0, idx[TILE + j], 0)),
            ],
            scratch_shapes=[
                pltpu.VMEM((QUAD - 1, width, columns), jnp.float32),
                pltpu.VMEM((len(NEAR_PAIRS), 16, LANES), jnp.float32),
            ],
        ),
        out_shape=[
            jax.ShapeDtypeStruct((1, LANES), jnp.float32),
            jax.ShapeDtypeStruct((QUAD - 1, steps * width, columns), jnp.bfloat16),
        ],
        compiler_params=pltpu.CompilerParams(vmem_limit_bytes=VMEM_LIMIT),
        cost_estimate=pl.CostEstimate(
            flops=6 * steps * width * rows * columns, bytes_accessed=12 * 2**20, transcendentals=0
        ),
        name="near_gram",
    )(idx, xt, *errors, *others)


def far_gram(idx, before, others, top, low, grads):
    _, width, rows = others[0].shape
    columns = top.shape[1]
    steps = len(others)
    return pl.pallas_call(
        functools.partial(far_kernel, steps),
        grid_spec=pltpu.PrefetchScalarGridSpec(
            num_scalar_prefetch=1,
            grid=(steps,),
            in_specs=[pl.BlockSpec((1, LANES), lambda j, idx: (0, 0))]
            + [once(top.shape, (0, 0))] * 2
            + [pl.BlockSpec((QUAD - 1, width, columns), lambda j, idx: (0, idx[TILE + j], 0))]
            + [once((1, width, rows), (QUAD - 2, 0, 0))] * steps,
            out_specs=[
                pl.BlockSpec((1, LANES), lambda j, idx: (0, 0)),
                pl.BlockSpec((width, columns), lambda j, idx: (idx[TILE + j], 0)),
            ],
            scratch_shapes=[
                pltpu.VMEM((width, columns), jnp.float32),
                pltpu.VMEM((len(FAR_PAIRS), 16, LANES), jnp.float32),
            ],
        ),
        out_shape=[
            jax.ShapeDtypeStruct((1, LANES), jnp.float32),
            jax.ShapeDtypeStruct((steps * width, columns), jnp.bfloat16),
        ],
        compiler_params=pltpu.CompilerParams(vmem_limit_bytes=VMEM_LIMIT),
        cost_estimate=pl.CostEstimate(
            flops=2 * steps * width * rows * columns, bytes_accessed=8 * 2**20, transcendentals=0
        ),
        name="far_gram",
    )(idx, before, top, low, grads, *others)


def merge_factors(gram_at):
    factors = [None] * QUAD
    for a, b in ((0, 1), (2, 3)):
        cross = gram_at(a, b)
        factors[a] = 1.0 - cross / (2.0 * gram_at(a, a))
        factors[b] = 1.0 - cross / (2.0 * gram_at(b, b))

    def product(left, right):
        return sum(factors[a] * factors[b] * gram_at(a, b) for a in left for b in right)

    cross = product((0, 1), (2, 3))
    first = 1.0 - cross / (2.0 * product((0, 1), (0, 1)))
    second = 1.0 - cross / (2.0 * product((2, 3), (2, 3)))
    return [factors[0] * first, factors[1] * first, factors[2] * second, factors[3] * second]


def merge_kernel(scale, idx, sums, grads, last, out):
    turn = idx[PLACE] * (QUAD + 1)
    factors = merge_factors(lambda a, b: sums[0, jnp.bitwise_xor(QUAD * a + b, turn)])
    total = (factors[QUAD - 1] * scale) * last[...].astype(jnp.float32)
    for k in range(QUAD - 1):
        total = total + (factors[k] * scale) * grads[k].astype(jnp.float32)
    out[...] = total.astype(out.dtype)


def merge(idx, flip, sums, grads, last, scale, per_block, width, at, columns):
    steps = grads.shape[1] // (2 * width)

    def tile(j, idx):
        bit = 1 - idx[BIT] if flip else idx[BIT]
        return (2 * (j // per_block) + bit) * per_block + j % per_block

    return pl.pallas_call(
        functools.partial(merge_kernel, scale),
        grid_spec=pltpu.PrefetchScalarGridSpec(
            num_scalar_prefetch=1,
            grid=(steps,),
            in_specs=[
                pl.BlockSpec(sums.shape, lambda j, idx: (0, 0), memory_space=pltpu.SMEM),
                pl.BlockSpec((QUAD - 1, width, columns), lambda j, idx: (0, tile(j, idx), at)),
                pl.BlockSpec((width, columns), lambda j, idx: (tile(j, idx), at)),
            ],
            out_specs=pl.BlockSpec((width, columns), lambda j, idx: (j, 0)),
        ),
        out_shape=jax.ShapeDtypeStruct((steps * width, columns), jnp.bfloat16),
        compiler_params=pltpu.CompilerParams(vmem_limit_bytes=VMEM_LIMIT),
        cost_estimate=pl.CostEstimate(
            flops=2 * QUAD * steps * width * columns,
            bytes_accessed=2 * (QUAD + 1) * steps * width * columns,
            transcendentals=0,
        ),
        name="merge",
    )(idx, sums, grads, last)


def partial_kernel(first_at, before, kept, received, out, acc):
    lane = lax.broadcasted_iota(jnp.int32, (1, LANES), 1)
    rows, columns = kept.shape

    def strip(i, sums):
        at = pl.ds(pl.multiple_of(i * 16, 16), 16)
        cross, mine, theirs = sums
        for c in range(columns // LANES):
            lanes = slice(c * LANES, (c + 1) * LANES)
            a = kept[at, lanes].astype(jnp.float32)
            b = received[at, lanes].astype(jnp.float32)
            cross, mine, theirs = cross + a * b, mine + a * a, theirs + b * b
        return cross, mine, theirs

    zero = jnp.zeros((16, LANES), jnp.float32)
    sums = lax.fori_loop(0, rows // 16, strip, (zero, zero, zero))
    result = before[...]
    for place, value in zip((0, 1 + first_at[0], 2 - first_at[0]), sums):
        total = jnp.sum(jnp.sum(value, axis=0, keepdims=True), axis=1, keepdims=True)
        result = result + jnp.where(lane == place, total, 0.0)
    out[...] = result


def partial_sums(bit, before, kept, received):
    return pl.pallas_call(
        partial_kernel,
        in_specs=[pl.BlockSpec(memory_space=pltpu.SMEM)] + [pl.BlockSpec(memory_space=pltpu.VMEM)] * 3,
        out_shape=jax.ShapeDtypeStruct((1, LANES), jnp.float32),
        scratch_shapes=[pltpu.VMEM((8, LANES), jnp.float32)],
        compiler_params=pltpu.CompilerParams(vmem_limit_bytes=VMEM_LIMIT),
        cost_estimate=pl.CostEstimate(flops=6 * kept.size, bytes_accessed=6 * kept.size, transcendentals=0),
        name="partial_sums",
    )(bit.reshape(1).astype(jnp.int32), before, kept, received)


def update_kernel(bit, sums, momentum, kept_0, kept_1, received_0, received_1, out):
    half = kept_0.shape[1]
    lower = bit[0] == 0
    lower_factor = 1.0 - sums[0, 0] / (2.0 * sums[0, 1])
    upper_factor = 1.0 - sums[0, 0] / (2.0 * sums[0, 2])
    factor = jnp.where(lower, lower_factor, upper_factor)
    other = jnp.where(lower, upper_factor, lower_factor)
    for at, a, b in ((slice(0, half), kept_0, received_0), (slice(half, 2 * half), kept_1, received_1)):
        out[:, at] = 0.9 * momentum[:, at] + (
            factor * a[...].astype(jnp.float32) + other * b[...].astype(jnp.float32)
        )


def update(bit, sums, momentum, kept, received):
    rows, columns = momentum.shape
    tile = math.gcd(rows, 128)
    spec = lambda width: pl.BlockSpec((tile, width), lambda i, *_: (i, 0))
    return pl.pallas_call(
        update_kernel,
        grid_spec=pltpu.PrefetchScalarGridSpec(
            num_scalar_prefetch=1,
            grid=(rows // tile,),
            in_specs=[pl.BlockSpec(sums.shape, lambda i, *_: (0, 0), memory_space=pltpu.SMEM), spec(columns)] + [spec(columns // 2)] * 4,
            out_specs=spec(columns),
        ),
        out_shape=jax.ShapeDtypeStruct(momentum.shape, jnp.float32),
        compiler_params=pltpu.CompilerParams(vmem_limit_bytes=VMEM_LIMIT),
        cost_estimate=pl.CostEstimate(
            flops=5 * momentum.size, bytes_accessed=14 * momentum.size, transcendentals=0
        ),
        name="update",
    )(bit.reshape(1).astype(jnp.int32), sums, momentum, *kept, *received)


def body(inputs, weight, targets, momentum):
    groups = lax.axis_size("dp")
    parts = lax.axis_size("tensor")
    depth = groups.bit_length() - 1
    me = lax.axis_index("dp")
    part = lax.axis_index("tensor")
    rows, depth_width = inputs.shape
    columns = weight.shape[1]
    block = depth_width // groups
    blocks = groups // QUAD
    width = blocks * block // parts
    per_block = block // width
    place = me % QUAD

    def columns_of(at, start, size):
        first = (QUAD * (start // block) + at) * block + start % block
        return lax.dynamic_slice(inputs, (0, first), (rows, size)).T

    slabs = [columns_of(place ^ k, part * width, width) for k in range(1, QUAD)]
    slabs, ready = lax.optimization_barrier((slabs, inputs))
    arrived = [exchange(s, "dp", k + 1) for k, s in enumerate(slabs)]

    top, low = forward(ready, weight, targets)
    arrived, top, low = lax.optimization_barrier((arrived, top, low))
    y_low, z_top = exchange(low, "dp", 1), exchange(top, "dp", 2)
    y_top, z_low = exchange(top, "dp", 1), exchange(low, "dp", 2)
    others, sources = [jnp.stack(arrived)], [part]
    own = jnp.concatenate([columns_of(place, b * block, block) for b in range(blocks)])
    part_grad = input_grad_part(weight, top, low)
    mask = parts // 2
    while mask:
        if mask == 1:
            others, own, part_grad, y_top, y_low, z_top, z_low = lax.optimization_barrier(
                (others, own, part_grad, y_top, y_low, z_top, z_low)
            )
        others = others + [exchange(o, "tensor", mask) for o in others]
        sources = sources + [s ^ mask for s in sources]
        mask //= 2
    far_top, far_low = exchange(z_top, "dp", 1), exchange(y_low, "dp", 2)

    bit = me >> 2 & 1
    idx = jnp.stack([place, bit] + sources).astype(jnp.int32)
    sums, grads = near_gram(idx, own, others, (top, low, y_top, y_low, z_top, z_low))
    sums, last = far_gram(idx, sums, others, far_top, far_low, grads)
    sums = total_over(sums, 2)
    half = columns // 2

    def merged_half(flip, h):
        return merge(idx, flip, sums, grads, last, rows**-0.5, per_block, width, h, half)

    sent = [merged_half(True, h) for h in range(2)]
    received = [exchange(s, "dp", 4) for s in sent]
    kept = [merged_half(False, h) for h in range(2)]
    summed = lax.psum_scatter(part_grad, "tensor", scatter_dimension=0, tiled=True)

    for level in range(2, depth):
        if level > 2:
            lower = bit == 0
            lower_factor = 1.0 - sums[0, 0] / (2.0 * sums[0, 1])
            upper_factor = 1.0 - sums[0, 0] / (2.0 * sums[0, 2])
            factor = jnp.where(lower, lower_factor, upper_factor)
            other = jnp.where(lower, upper_factor, lower_factor)
            merged = [
                factor * a.astype(jnp.float32) + other * b.astype(jnp.float32) for a, b in zip(kept, received)
            ]
            bit = me >> level & 1
            paired = [v.reshape(v.shape[0] // (2 * block), 2, block, v.shape[1]) for v in merged]
            kept = [jnp.where(bit == 0, v[:, 0], v[:, 1]).reshape(-1, v.shape[-1]) for v in paired]
            sent = [jnp.where(bit == 0, v[:, 1], v[:, 0]).reshape(-1, v.shape[-1]) for v in paired]
            received = [exchange(s.astype(jnp.bfloat16), "dp", 2**level) for s in sent]
        sums = jnp.zeros((1, LANES), jnp.float32)
        for a, b in zip(kept, received):
            sums = partial_sums(bit, sums, a, b)
        sums = total_over(sums, level + 1)
    new_momentum = update(bit, sums, momentum, kept, received)
    return (summed, new_momentum, jnp.sqrt(sums[0, 1:3]) / depth_width)


def solution(mesh):
    return jax.shard_map(
        body,
        mesh=mesh,
        in_specs=(P("dp", None), P(None, "tensor"), P("dp", "tensor"), P("dp", "tensor")),
        out_specs=(P("tensor", "dp"), P("dp", "tensor"), P()),
        check_vma=False,
    )
```

```python
import functools
import math

import jax
import jax.numpy as jnp
from jax import lax
from jax.experimental import pallas as pl
from jax.experimental.pallas import tpu as pltpu
from jax.sharding import PartitionSpec as P

QUAD = 4
LANES = 128
SMALL = pl.CostEstimate(flops=1, bytes_accessed=1, transcendentals=0)
VMEM_LIMIT = 18 * 2**20
FULL_VMEM = 44 * 2**20


def in_hbm(value):
    return pltpu.with_memory_space_constraint(value, pltpu.HBM)


def exchange(value, axis, mask):
    pairs = [(source, source ^ mask) for source in range(lax.axis_size(axis))]
    return lax.ppermute(value, axis, pairs)


def total_over(value, dp_bits):
    mask = 1
    while mask < lax.axis_size("tensor"):
        value = value + exchange(value, "tensor", mask)
        mask *= 2
    for bit in range(dp_bits):
        value = value + exchange(value, "dp", 2**bit)
    return value


def dot(a, b):
    return jnp.dot(a, b, preferred_element_type=jnp.float32)


def pair_sums(pairs, strips, rows, load, acc):
    def strip(i, sums):
        sums = list(sums)
        for tile in load(i * rows):
            for n, (a, b) in enumerate(pairs):
                sums[n] = sums[n] + tile[a] * tile[b]
        return tuple(sums)

    sums = lax.fori_loop(0, strips, strip, tuple(acc[n] for n in range(len(pairs))))
    for n in range(len(pairs)):
        acc[n] = sums[n]


def place_sums(place, pairs, acc, result):
    lane = lax.broadcasted_iota(jnp.int32, (1, LANES), 1)
    turn = place * (QUAD + 1)
    for n, (a, b) in enumerate(pairs):
        value = jnp.sum(jnp.sum(acc[n], axis=0, keepdims=True), axis=1, keepdims=True)
        first = jnp.bitwise_xor(QUAD * a + b, turn)
        second = jnp.bitwise_xor(QUAD * b + a, turn)
        result = jnp.where((lane == first) | (lane == second), value, result)
    return result


def lanes_of(columns):
    return [slice(c, c + LANES) for c in range(0, columns, LANES)]


NEAR_PAIRS = [(0, 1), (0, 2), (1, 1), (1, 2), (2, 2)]
FAR_PAIRS = [(a, QUAD - 1) for a in range(QUAD)]


def forward_kernel(x, w, targets, out):
    out[...] = (dot(x[...], w[...]) - targets[...].astype(jnp.float32)).astype(out.dtype)


def forward(inputs, weight, targets, part, parts):
    rows, inner = inputs.shape
    columns = weight.shape[1] // parts
    tile = math.gcd(columns, 256)
    first = part * columns // tile
    return pl.pallas_call(
        forward_kernel,
        grid=(columns // tile,),
        in_specs=[
            pl.BlockSpec((rows, inner), lambda j: (0, 0), pipeline_mode=pl.Buffered(1)),
            pl.BlockSpec((inner, tile), lambda j: (0, first + j)),
            pl.BlockSpec((rows, tile), lambda j: (0, first + j)),
        ],
        out_specs=pl.BlockSpec((rows, tile), lambda j: (0, j)),
        out_shape=jax.ShapeDtypeStruct((rows, columns), jnp.bfloat16),
        compiler_params=pltpu.CompilerParams(vmem_limit_bytes=FULL_VMEM),
        cost_estimate=SMALL,
        name="forward",
    )(inputs, weight, targets)


def input_grad_kernel(w, left, right, out):
    half = left.shape[1]
    total = 0.0
    for at, error in ((0, left), (half, right)):
        total = total + lax.dot_general(
            w[:, at:at + half], error[...], (((1,), (1,)), ((), ())), preferred_element_type=jnp.float32
        )
    out[...] = total.astype(out.dtype)


def input_grad_part(weight, left, right):
    inner, columns = weight.shape
    rows = left.shape[0]
    tile = math.gcd(inner, 1024)
    whole = pl.BlockSpec(left.shape, lambda j: (0, 0), pipeline_mode=pl.Buffered(1))
    return pl.pallas_call(
        input_grad_kernel,
        grid=(inner // tile,),
        in_specs=[pl.BlockSpec((tile, columns), lambda j: (j, 0)), whole, whole],
        out_specs=pl.BlockSpec((tile, rows), lambda j: (j, 0)),
        out_shape=pltpu.HBM((inner, rows), jnp.bfloat16),
        compiler_params=pltpu.CompilerParams(vmem_limit_bytes=FULL_VMEM),
        cost_estimate=SMALL,
        name="input_grad_part",
    )(weight, left, right)


def fill(tile, xt, left, right):
    half = left.shape[1]
    tile[:, :half] = dot(xt, left[...])
    tile[:, half:] = dot(xt, right[...])


STRIP = 16


def strip_at(first):
    return pl.ds(pl.multiple_of(first, STRIP), STRIP)


def own_kernel(idx, x, left, right, out, grads, tile, acc):
    step = pl.program_id(0)
    half = left.shape[1]

    @pl.when(step == 0)
    def _():
        acc[...] = jnp.zeros_like(acc)

    for at, error in ((0, left), (half, right)):
        tile[:, at:at + half] = lax.dot_general(
            x[...], error[...], (((0,), (0,)), ((), ())), preferred_element_type=jnp.float32
        )

    def load(first):
        at = strip_at(first)
        for lanes in lanes_of(tile.shape[1]):
            mine = tile[at, lanes]
            grads[at, lanes] = mine.astype(grads.dtype)
            yield [mine]

    pair_sums([(0, 0)], tile.shape[0] // STRIP, STRIP, load, acc)

    @pl.when(step == pl.num_programs(0) - 1)
    def _():
        out[...] = place_sums(idx[PLACE], [(0, 0)], acc, jnp.zeros((1, LANES), jnp.float32))


def own_gram(idx, inputs, left, right, width, block):
    rows, inner = inputs.shape
    columns = 2 * left.shape[1]
    steps = inner // (QUAD * width)
    per_block = block // width

    def tile(j, idx):
        return (QUAD * (j // per_block) + idx[PLACE]) * per_block + j % per_block

    return pl.pallas_call(
        own_kernel,
        grid_spec=pltpu.PrefetchScalarGridSpec(
            num_scalar_prefetch=1,
            grid=(steps,),
            in_specs=[pl.BlockSpec((rows, width), lambda j, idx: (0, tile(j, idx)))]
            + [once(left.shape, (0, 0))] * 2,
            out_specs=[
                pl.BlockSpec((1, LANES), lambda j, idx: (0, 0)),
                pl.BlockSpec((width, columns), lambda j, idx: (j, 0)),
            ],
            scratch_shapes=[
                pltpu.VMEM((width, columns), jnp.float32),
                pltpu.VMEM((1, 16, LANES), jnp.float32),
            ],
        ),
        out_shape=[
            jax.ShapeDtypeStruct((1, LANES), jnp.float32),
            jax.ShapeDtypeStruct((steps * width, columns), jnp.bfloat16),
        ],
        compiler_params=pltpu.CompilerParams(vmem_limit_bytes=FULL_VMEM),
        cost_estimate=SMALL,
        name="own_gram",
    )(idx, inputs, left, right)


def near_kernel(pieces, idx, before, own, y_left, y_right, z_left, z_right, *refs):
    others, (out, grads, tiles, acc) = refs[:pieces], refs[pieces:]
    width = tiles.shape[1]
    acc[...] = jnp.zeros_like(acc)
    for q, other in enumerate(others):
        fill(tiles.at[0], other[0], y_left, y_right)
        fill(tiles.at[1], other[1], z_left, z_right)

        def load(first):
            at, there = strip_at(first), strip_at(idx[TILE + q] * width + first)
            for lanes in lanes_of(tiles.shape[2]):
                tile = [tiles[k, at, lanes] for k in range(QUAD - 2)]
                for k in range(QUAD - 2):
                    grads[k, there, lanes] = tile[k].astype(grads.dtype)
                yield [own[there, lanes].astype(jnp.float32)] + tile

        pair_sums(NEAR_PAIRS, width // STRIP, STRIP, load, acc)
    out[...] = place_sums(idx[PLACE], NEAR_PAIRS, acc, before[...])


def far_kernel(pieces, idx, before, left, right, own, grads, *refs):
    others, (out, last, tile, acc) = refs[:pieces], refs[pieces:]
    width = tile.shape[0]
    acc[...] = jnp.zeros_like(acc)
    for q, other in enumerate(others):
        fill(tile, other[QUAD - 2], left, right)

        def load(first):
            at, there = strip_at(first), strip_at(idx[TILE + q] * width + first)
            for lanes in lanes_of(tile.shape[1]):
                mine = tile[at, lanes]
                last[there, lanes] = mine.astype(last.dtype)
                three = [own[there, lanes]] + [grads[k, there, lanes] for k in range(QUAD - 2)]
                yield [v.astype(jnp.float32) for v in three] + [mine]

        pair_sums(FAR_PAIRS, width // STRIP, STRIP, load, acc)
    out[...] = place_sums(idx[PLACE], FAR_PAIRS, acc, before[...])


def once(shape, at):
    return pl.BlockSpec(shape, lambda j, idx: at, pipeline_mode=pl.Buffered(1))


PLACE, BIT, TILE = 0, 1, 2


def in_place(kernel, inputs, out_shape, scratch_shapes, name):
    return pl.pallas_call(
        kernel,
        in_specs=[pl.BlockSpec(memory_space=m) for m, _ in inputs],
        out_specs=[pl.BlockSpec(memory_space=pltpu.VMEM)] * len(out_shape),
        out_shape=out_shape,
        scratch_shapes=scratch_shapes,
        compiler_params=pltpu.CompilerParams(vmem_limit_bytes=VMEM_LIMIT),
        cost_estimate=SMALL,
        name=name,
    )(*[v for _, v in inputs])


def near_gram(idx, before, own, others, errors):
    _, width, _ = others[0].shape
    rows, columns = own.shape
    return in_place(
        functools.partial(near_kernel, len(others)),
        [(pltpu.SMEM, idx)] + [(pltpu.VMEM, v) for v in (before, own, *errors, *others)],
        [
            jax.ShapeDtypeStruct((1, LANES), jnp.float32),
            jax.ShapeDtypeStruct((QUAD - 2, rows, columns), jnp.bfloat16),
        ],
        [
            pltpu.VMEM((QUAD - 2, width, columns), jnp.float32),
            pltpu.VMEM((len(NEAR_PAIRS), STRIP, LANES), jnp.float32),
        ],
        "near_gram",
    )


def far_gram(idx, before, own, others, left, right, grads):
    _, width, _ = others[0].shape
    rows, columns = own.shape
    return in_place(
        functools.partial(far_kernel, len(others)),
        [(pltpu.SMEM, idx)] + [(pltpu.VMEM, v) for v in (before, left, right, own, grads, *others)],
        [
            jax.ShapeDtypeStruct((1, LANES), jnp.float32),
            jax.ShapeDtypeStruct((rows, columns), jnp.bfloat16),
        ],
        [
            pltpu.VMEM((width, columns), jnp.float32),
            pltpu.VMEM((len(FAR_PAIRS), STRIP, LANES), jnp.float32),
        ],
        "far_gram",
    )


def merge_factors(gram_at):
    factors = [None] * QUAD
    for a, b in ((0, 1), (2, 3)):
        cross = gram_at(a, b)
        factors[a] = 1.0 - cross / (2.0 * gram_at(a, a))
        factors[b] = 1.0 - cross / (2.0 * gram_at(b, b))

    def product(left, right):
        return sum(factors[a] * factors[b] * gram_at(a, b) for a in left for b in right)

    cross = product((0, 1), (2, 3))
    first = 1.0 - cross / (2.0 * product((0, 1), (0, 1)))
    second = 1.0 - cross / (2.0 * product((2, 3), (2, 3)))
    return [factors[0] * first, factors[1] * first, factors[2] * second, factors[3] * second]


def merge_kernel(scale, flip, per_block, width, at, idx, sums, own, grads, last, out):
    turn = idx[PLACE] * (QUAD + 1)
    factors = merge_factors(lambda a, b: sums[0, jnp.bitwise_xor(QUAD * a + b, turn)])
    factors = [factor * scale for factor in factors]
    bit = 1 - idx[BIT] if flip else idx[BIT]
    columns = out.shape[1]
    for j in range(out.shape[0] // width):
        tile = (2 * (j // per_block) + bit) * per_block + j % per_block

        def strip(i, carry):
            there, here = strip_at(tile * width + i * STRIP), strip_at(j * width + i * STRIP)
            for lanes in lanes_of(columns):
                from_lanes = slice(at * columns + lanes.start, at * columns + lanes.stop)
                four = (own[there, from_lanes], grads[0, there, from_lanes])
                four += (grads[1, there, from_lanes], last[there, from_lanes])
                total = factors[0] * four[0].astype(jnp.float32)
                for factor, value in zip(factors[1:], four[1:]):
                    total = total + factor * value.astype(jnp.float32)
                out[here, lanes] = total.astype(out.dtype)
            return carry

        lax.fori_loop(0, width // STRIP, strip, 0)


def merge(idx, flip, sums, own, grads, last, scale, per_block, width, at, columns):
    return in_place(
        functools.partial(merge_kernel, scale, flip, per_block, width, at),
        [(pltpu.SMEM, idx), (pltpu.SMEM, sums)] + [(pltpu.VMEM, v) for v in (own, grads, last)],
        [jax.ShapeDtypeStruct((own.shape[0] // 2, columns), jnp.bfloat16)],
        [],
        "merge",
    )[0]


def partial_kernel(first_at, before, kept, received, out, acc):
    lane = lax.broadcasted_iota(jnp.int32, (1, LANES), 1)
    rows, columns = kept.shape

    def strip(i, sums):
        at = pl.ds(pl.multiple_of(i * 16, 16), 16)
        cross, mine, theirs = sums
        for c in range(columns // LANES):
            lanes = slice(c * LANES, (c + 1) * LANES)
            a = kept[at, lanes].astype(jnp.float32)
            b = received[at, lanes].astype(jnp.float32)
            cross, mine, theirs = cross + a * b, mine + a * a, theirs + b * b
        return cross, mine, theirs

    zero = jnp.zeros((16, LANES), jnp.float32)
    sums = lax.fori_loop(0, rows // 16, strip, (zero, zero, zero))
    result = before[...]
    for place, value in zip((0, 1 + first_at[0], 2 - first_at[0]), sums):
        total = jnp.sum(jnp.sum(value, axis=0, keepdims=True), axis=1, keepdims=True)
        result = result + jnp.where(lane == place, total, 0.0)
    out[...] = result


def partial_sums(bit, before, kept, received):
    return pl.pallas_call(
        partial_kernel,
        in_specs=[pl.BlockSpec(memory_space=pltpu.SMEM)] + [pl.BlockSpec(memory_space=pltpu.VMEM)] * 3,
        out_shape=jax.ShapeDtypeStruct((1, LANES), jnp.float32),
        scratch_shapes=[pltpu.VMEM((8, LANES), jnp.float32)],
        compiler_params=pltpu.CompilerParams(vmem_limit_bytes=VMEM_LIMIT),
        cost_estimate=SMALL,
        name="partial_sums",
    )(bit.reshape(1).astype(jnp.int32), before, kept, received)


def update_kernel(bit, sums, momentum, kept_0, kept_1, received_0, received_1, out):
    half = kept_0.shape[1]
    lower = bit[0] == 0
    lower_factor = 1.0 - sums[0, 0] / (2.0 * sums[0, 1])
    upper_factor = 1.0 - sums[0, 0] / (2.0 * sums[0, 2])
    factor = jnp.where(lower, lower_factor, upper_factor)
    other = jnp.where(lower, upper_factor, lower_factor)
    for at, a, b in ((slice(0, half), kept_0, received_0), (slice(half, 2 * half), kept_1, received_1)):
        out[:, at] = 0.9 * momentum[:, at] + (
            factor * a[...].astype(jnp.float32) + other * b[...].astype(jnp.float32)
        )


def update(bit, sums, momentum, kept, received):
    rows, columns = momentum.shape
    tile = math.gcd(rows, 128)
    spec = lambda width: pl.BlockSpec((tile, width), lambda i, *_: (i, 0))
    return pl.pallas_call(
        update_kernel,
        grid_spec=pltpu.PrefetchScalarGridSpec(
            num_scalar_prefetch=1,
            grid=(rows // tile,),
            in_specs=[pl.BlockSpec(sums.shape, lambda i, *_: (0, 0), memory_space=pltpu.SMEM), spec(columns)] + [spec(columns // 2)] * 4,
            out_specs=spec(columns),
        ),
        out_shape=jax.ShapeDtypeStruct(momentum.shape, jnp.float32),
        compiler_params=pltpu.CompilerParams(vmem_limit_bytes=VMEM_LIMIT),
        cost_estimate=SMALL,
        name="update",
    )(bit.reshape(1).astype(jnp.int32), sums, momentum, *kept, *received)


def body(inputs, weight, targets, momentum):
    groups = lax.axis_size("dp")
    parts = lax.axis_size("tensor")
    depth = groups.bit_length() - 1
    me = lax.axis_index("dp")
    part = lax.axis_index("tensor")
    rows, depth_width = inputs.shape
    columns = weight.shape[1]
    block = depth_width // groups
    width = depth_width // QUAD // parts
    per_block = block // width
    place = me % QUAD

    def columns_of(at, start, size):
        first = (QUAD * (start // block) + at) * block + start % block
        return lax.dynamic_slice(inputs, (0, first), (rows, size)).T

    slabs = [columns_of(place ^ k, part * width, width) for k in range(1, QUAD)]
    slabs, ready = lax.optimization_barrier((slabs, inputs))
    arrived = [exchange(s, "dp", k + 1) for k, s in enumerate(slabs)]

    left = forward(ready, in_hbm(weight), targets, 0, 2)
    arrived[:2], left, ready = lax.optimization_barrier((arrived[:2], left, ready))
    y_left, z_left = exchange(left, "dp", 1), exchange(left, "dp", 2)
    right = forward(ready, in_hbm(weight), targets, 1, 2)
    y_right, z_right = exchange(right, "dp", 1), exchange(right, "dp", 2)
    others, sources = [jnp.stack(arrived)], [part]
    mask = parts // 2
    while mask:
        sources = sources + [s ^ mask for s in sources]
        mask //= 2
    bit = me >> 2 & 1
    idx = jnp.stack([place, bit] + sources).astype(jnp.int32)
    sums, own = own_gram(idx, in_hbm(inputs), left, right, width, block)
    left, right, y_left, z_left, own = lax.optimization_barrier((left, right, y_left, z_left, own))
    part_grad = input_grad_part(in_hbm(weight), left, right)
    mask = parts // 2
    while mask:
        if mask == 1:
            others, part_grad, y_right, z_right, z_left = lax.optimization_barrier(
                (others, part_grad, y_right, z_right, z_left)
            )
        others = others + [exchange(o, "tensor", mask) for o in others]
        mask //= 2
    far_left, far_right = exchange(z_left, "dp", 1), exchange(y_right, "dp", 2)

    sums, grads = near_gram(idx, sums, own, others, (y_left, y_right, z_left, z_right))
    sums, last = far_gram(idx, sums, own, others, far_left, far_right, grads)
    sums = total_over(sums, 2)
    half = columns // 2

    def merged_half(flip, h):
        return merge(idx, flip, sums, own, grads, last, rows**-0.5, per_block, width, h, half)

    sent = [merged_half(True, h) for h in range(2)]
    received = [exchange(s, "dp", 4) for s in sent]
    _, sums = lax.optimization_barrier((sent, sums))
    kept = [merged_half(False, h) for h in range(2)]
    summed = lax.psum_scatter(part_grad, "tensor", scatter_dimension=0, tiled=True)

    for level in range(2, depth):
        if level > 2:
            lower = bit == 0
            lower_factor = 1.0 - sums[0, 0] / (2.0 * sums[0, 1])
            upper_factor = 1.0 - sums[0, 0] / (2.0 * sums[0, 2])
            factor = jnp.where(lower, lower_factor, upper_factor)
            other = jnp.where(lower, upper_factor, lower_factor)
            merged = [
                factor * a.astype(jnp.float32) + other * b.astype(jnp.float32) for a, b in zip(kept, received)
            ]
            bit = me >> level & 1
            paired = [v.reshape(v.shape[0] // (2 * block), 2, block, v.shape[1]) for v in merged]
            kept = [jnp.where(bit == 0, v[:, 0], v[:, 1]).reshape(-1, v.shape[-1]) for v in paired]
            sent = [jnp.where(bit == 0, v[:, 1], v[:, 0]).reshape(-1, v.shape[-1]) for v in paired]
            received = [exchange(s.astype(jnp.bfloat16), "dp", 2**level) for s in sent]
        sums = jnp.zeros((1, LANES), jnp.float32)
        for a, b in zip(kept, received):
            sums = partial_sums(bit, sums, a, b)
        sums = total_over(sums, level + 1)
    new_momentum = update(bit, sums, momentum, kept, received)
    return (summed, new_momentum, jnp.sqrt(sums[0, 1:3]) / depth_width)


def solution(mesh):
    return jax.shard_map(
        body,
        mesh=mesh,
        in_specs=(P("dp", None), P(None, "tensor"), P("dp", "tensor"), P("dp", "tensor")),
        out_specs=(P("tensor", "dp"), P("dp", "tensor"), P()),
        check_vma=False,
    )
```

```python
import functools
import math

import jax
import jax.numpy as jnp
from jax import lax
from jax.experimental import pallas as pl
from jax.experimental.pallas import tpu as pltpu
from jax.sharding import PartitionSpec as P

QUAD = 4
LANES = 128
SMALL = pl.CostEstimate(flops=1, bytes_accessed=1, transcendentals=0)
VMEM_LIMIT = 18 * 2**20
FULL_VMEM = 44 * 2**20


def in_hbm(value):
    return pltpu.with_memory_space_constraint(value, pltpu.HBM)


def exchange(value, axis, mask):
    pairs = [(source, source ^ mask) for source in range(lax.axis_size(axis))]
    return lax.ppermute(value, axis, pairs)


def total_over(value, dp_bits):
    hops = [("tensor", 1)] + [("dp", 2**bit) for bit in range(dp_bits)]
    mask = 2
    while mask < lax.axis_size("tensor"):
        hops.append(("tensor", mask))
        mask *= 2
    for axis, mask in hops:
        value = value + exchange(value, axis, mask)
    return value


def dot(a, b):
    return jnp.dot(a, b, preferred_element_type=jnp.float32)


def pair_sums(pairs, strips, rows, load, acc):
    def strip(i, sums):
        sums = list(sums)
        for tile in load(i * rows):
            for n, (a, b) in enumerate(pairs):
                sums[n] = sums[n] + tile[a] * tile[b]
        return tuple(sums)

    sums = lax.fori_loop(0, strips, strip, tuple(acc[n] for n in range(len(pairs))))
    for n in range(len(pairs)):
        acc[n] = sums[n]


def place_sums(place, pairs, acc, result):
    lane = lax.broadcasted_iota(jnp.int32, (1, LANES), 1)
    turn = place * (QUAD + 1)
    for n, (a, b) in enumerate(pairs):
        value = jnp.sum(jnp.sum(acc[n], axis=0, keepdims=True), axis=1, keepdims=True)
        first = jnp.bitwise_xor(QUAD * a + b, turn)
        second = jnp.bitwise_xor(QUAD * b + a, turn)
        result = jnp.where((lane == first) | (lane == second), value, result)
    return result


def lanes_of(columns):
    return [slice(c, c + LANES) for c in range(0, columns, LANES)]


NEAR_PAIRS = [(0, 1), (0, 2), (1, 1), (1, 2), (2, 2)]
FAR_PAIRS = [(a, QUAD - 1) for a in range(QUAD)]


def forward_kernel(x, w, targets, out):
    out[...] = (dot(x[...], w[...]) - targets[...].astype(jnp.float32)).astype(out.dtype)


def forward(inputs, weight, targets, part, parts):
    rows, inner = inputs.shape
    columns = weight.shape[1] // parts
    tile = math.gcd(columns, 256)
    first = part * columns // tile
    return pl.pallas_call(
        forward_kernel,
        grid=(columns // tile,),
        in_specs=[
            pl.BlockSpec((rows, inner), lambda j: (0, 0), pipeline_mode=pl.Buffered(1)),
            pl.BlockSpec((inner, tile), lambda j: (0, first + j)),
            pl.BlockSpec((rows, tile), lambda j: (0, first + j)),
        ],
        out_specs=pl.BlockSpec((rows, tile), lambda j: (0, j)),
        out_shape=jax.ShapeDtypeStruct((rows, columns), jnp.bfloat16),
        compiler_params=pltpu.CompilerParams(vmem_limit_bytes=FULL_VMEM),
        cost_estimate=SMALL,
        name="forward",
    )(inputs, weight, targets)


def input_grad_kernel(idx, w_send, w_keep, left, right, send, keep):
    half = left.shape[1]
    for w, out in ((w_send, send), (w_keep, keep)):
        total = 0.0
        for at, error in ((0, left), (half, right)):
            total = total + lax.dot_general(
                w[:, at:at + half],
                error[...],
                (((1,), (1,)), ((), ())),
                preferred_element_type=jnp.float32,
            )
        out[0] = total.astype(out.dtype)


def input_grad_part(idx, parts, weight, left, right):
    inner, columns = weight.shape
    rows = left.shape[0]
    block = inner // parts
    tile = math.gcd(block, 512)
    per_block = block // tile

    def blocks_of(flip):
        def at(j, idx):
            parity = 1 - idx[PARITY] if flip else idx[PARITY]
            return ((2 * (j // per_block) + parity) * per_block + j % per_block, 0)

        return pl.BlockSpec((tile, columns), at)

    out = pltpu.HBM((parts // 2, block, rows), jnp.bfloat16)
    return pl.pallas_call(
        input_grad_kernel,
        grid_spec=pltpu.PrefetchScalarGridSpec(
            num_scalar_prefetch=1,
            grid=(parts // 2 * per_block,),
            in_specs=[blocks_of(True), blocks_of(False)] + [once(left.shape, (0, 0))] * 2,
            out_specs=[pl.BlockSpec((1, tile, rows), lambda j, idx: (j // per_block, j % per_block, 0))] * 2,
        ),
        out_shape=[out, out],
        compiler_params=pltpu.CompilerParams(vmem_limit_bytes=VMEM_LIMIT),
        cost_estimate=SMALL,
        name="input_grad_part",
    )(idx, weight, weight, left, right)


def fill(tile, xt, left, right):
    half = left.shape[1]
    tile[:, :half] = dot(xt, left[...])
    tile[:, half:] = dot(xt, right[...])


STRIP = 16


def strip_at(first):
    return pl.ds(pl.multiple_of(first, STRIP), STRIP)


def own_kernel(idx, x, left, right, out, grads, tile, acc):
    step = pl.program_id(0)
    half = left.shape[1]

    @pl.when(step == 0)
    def _():
        acc[...] = jnp.zeros_like(acc)

    for at, error in ((0, left), (half, right)):
        tile[:, at:at + half] = lax.dot_general(
            x[...], error[...], (((0,), (0,)), ((), ())), preferred_element_type=jnp.float32
        )

    def load(first):
        at = strip_at(first)
        for lanes in lanes_of(tile.shape[1]):
            mine = tile[at, lanes]
            grads[at, lanes] = mine.astype(grads.dtype)
            yield [mine]

    pair_sums([(0, 0)], tile.shape[0] // STRIP, STRIP, load, acc)

    @pl.when(step == pl.num_programs(0) - 1)
    def _():
        out[...] = place_sums(idx[PLACE], [(0, 0)], acc, jnp.zeros((1, LANES), jnp.float32))


def own_gram(idx, inputs, left, right, width, block):
    rows, inner = inputs.shape
    columns = 2 * left.shape[1]
    steps = inner // (QUAD * width)
    per_block = block // width

    def tile(j, idx):
        return (QUAD * (j // per_block) + idx[PLACE]) * per_block + j % per_block

    return pl.pallas_call(
        own_kernel,
        grid_spec=pltpu.PrefetchScalarGridSpec(
            num_scalar_prefetch=1,
            grid=(steps,),
            in_specs=[pl.BlockSpec((rows, width), lambda j, idx: (0, tile(j, idx)))]
            + [once(left.shape, (0, 0))] * 2,
            out_specs=[
                pl.BlockSpec((1, LANES), lambda j, idx: (0, 0)),
                pl.BlockSpec((width, columns), lambda j, idx: (j, 0)),
            ],
            scratch_shapes=[
                pltpu.VMEM((width, columns), jnp.float32),
                pltpu.VMEM((1, 16, LANES), jnp.float32),
            ],
        ),
        out_shape=[
            jax.ShapeDtypeStruct((1, LANES), jnp.float32),
            jax.ShapeDtypeStruct((steps * width, columns), jnp.bfloat16),
        ],
        compiler_params=pltpu.CompilerParams(vmem_limit_bytes=VMEM_LIMIT),
        cost_estimate=SMALL,
        name="own_gram",
    )(idx, inputs, left, right)


def near_kernel(pieces, idx, before, own, y_left, y_right, z_left, z_right, *refs):
    others, (out, grads, tiles, acc) = refs[:pieces], refs[pieces:]
    width = tiles.shape[1]
    acc[...] = jnp.zeros_like(acc)
    for q, other in enumerate(others):
        fill(tiles.at[0], other[0], y_left, y_right)
        fill(tiles.at[1], other[1], z_left, z_right)

        def load(first):
            at, there = strip_at(first), strip_at(idx[TILE + q] * width + first)
            for lanes in lanes_of(tiles.shape[2]):
                tile = [tiles[k, at, lanes] for k in range(QUAD - 2)]
                for k in range(QUAD - 2):
                    grads[k, there, lanes] = tile[k].astype(grads.dtype)
                yield [own[there, lanes].astype(jnp.float32)] + tile

        pair_sums(NEAR_PAIRS, width // STRIP, STRIP, load, acc)
    out[...] = place_sums(idx[PLACE], NEAR_PAIRS, acc, before[...])


def far_kernel(pieces, idx, before, left, right, own, grads, *refs):
    others, (out, last, tile, acc) = refs[:pieces], refs[pieces:]
    width = tile.shape[0]
    acc[...] = jnp.zeros_like(acc)
    for q, other in enumerate(others):
        fill(tile, other[...], left, right)

        def load(first):
            at, there = strip_at(first), strip_at(idx[TILE + q] * width + first)
            for lanes in lanes_of(tile.shape[1]):
                mine = tile[at, lanes]
                last[there, lanes] = mine.astype(last.dtype)
                three = [own[there, lanes]] + [grads[k, there, lanes] for k in range(QUAD - 2)]
                yield [v.astype(jnp.float32) for v in three] + [mine]

        pair_sums(FAR_PAIRS, width // STRIP, STRIP, load, acc)
    out[...] = place_sums(idx[PLACE], FAR_PAIRS, acc, before[...])


def once(shape, at):
    return pl.BlockSpec(shape, lambda j, idx: at, pipeline_mode=pl.Buffered(1))


PLACE, BIT, PARITY, TILE = 0, 1, 2, 3


def in_place(kernel, inputs, out_shape, scratch_shapes, name):
    return pl.pallas_call(
        kernel,
        in_specs=[pl.BlockSpec(memory_space=m) for m, _ in inputs],
        out_specs=[pl.BlockSpec(memory_space=pltpu.VMEM)] * len(out_shape),
        out_shape=out_shape,
        scratch_shapes=scratch_shapes,
        compiler_params=pltpu.CompilerParams(vmem_limit_bytes=VMEM_LIMIT),
        cost_estimate=SMALL,
        name=name,
    )(*[v for _, v in inputs])


def near_gram(idx, before, own, others, errors):
    width = others[0].shape[-2]
    rows, columns = own.shape
    return in_place(
        functools.partial(near_kernel, len(others)),
        [(pltpu.SMEM, idx)] + [(pltpu.VMEM, v) for v in (before, own, *errors, *others)],
        [
            jax.ShapeDtypeStruct((1, LANES), jnp.float32),
            jax.ShapeDtypeStruct((QUAD - 2, rows, columns), jnp.bfloat16),
        ],
        [
            pltpu.VMEM((QUAD - 2, width, columns), jnp.float32),
            pltpu.VMEM((len(NEAR_PAIRS), STRIP, LANES), jnp.float32),
        ],
        "near_gram",
    )


def far_gram(idx, before, own, others, left, right, grads):
    width = others[0].shape[-2]
    rows, columns = own.shape
    return in_place(
        functools.partial(far_kernel, len(others)),
        [(pltpu.SMEM, idx)] + [(pltpu.VMEM, v) for v in (before, left, right, own, grads, *others)],
        [
            jax.ShapeDtypeStruct((1, LANES), jnp.float32),
            jax.ShapeDtypeStruct((rows, columns), jnp.bfloat16),
        ],
        [
            pltpu.VMEM((width, columns), jnp.float32),
            pltpu.VMEM((len(FAR_PAIRS), STRIP, LANES), jnp.float32),
        ],
        "far_gram",
    )


def merge_factors(gram_at):
    factors = [None] * QUAD
    for a, b in ((0, 1), (2, 3)):
        cross = gram_at(a, b)
        factors[a] = 1.0 - cross / (2.0 * gram_at(a, a))
        factors[b] = 1.0 - cross / (2.0 * gram_at(b, b))

    def product(left, right):
        return sum(factors[a] * factors[b] * gram_at(a, b) for a in left for b in right)

    cross = product((0, 1), (2, 3))
    first = 1.0 - cross / (2.0 * product((0, 1), (0, 1)))
    second = 1.0 - cross / (2.0 * product((2, 3), (2, 3)))
    return [factors[0] * first, factors[1] * first, factors[2] * second, factors[3] * second]


def merge_kernel(scale, flip, per_block, width, at, idx, sums, own, grads, last, out):
    turn = idx[PLACE] * (QUAD + 1)
    factors = merge_factors(lambda a, b: sums[0, jnp.bitwise_xor(QUAD * a + b, turn)])
    factors = [factor * scale for factor in factors]
    bit = 1 - idx[BIT] if flip else idx[BIT]
    columns = out.shape[1]
    for j in range(out.shape[0] // width):
        tile = (2 * (j // per_block) + bit) * per_block + j % per_block

        def strip(i, carry):
            there, here = strip_at(tile * width + i * STRIP), strip_at(j * width + i * STRIP)
            for lanes in lanes_of(columns):
                from_lanes = slice(at * columns + lanes.start, at * columns + lanes.stop)
                four = (own[there, from_lanes], grads[0, there, from_lanes])
                four += (grads[1, there, from_lanes], last[there, from_lanes])
                total = factors[0] * four[0].astype(jnp.float32)
                for factor, value in zip(factors[1:], four[1:]):
                    total = total + factor * value.astype(jnp.float32)
                out[here, lanes] = total.astype(out.dtype)
            return carry

        lax.fori_loop(0, width // STRIP, strip, 0)


def merge(idx, flip, sums, own, grads, last, scale, per_block, width, at, columns):
    return in_place(
        functools.partial(merge_kernel, scale, flip, per_block, width, at),
        [(pltpu.SMEM, idx), (pltpu.SMEM, sums)] + [(pltpu.VMEM, v) for v in (own, grads, last)],
        [jax.ShapeDtypeStruct((own.shape[0] // 2, columns), jnp.bfloat16)],
        [],
        "merge",
    )[0]


def partial_kernel(first_at, before, kept, received, out, acc):
    lane = lax.broadcasted_iota(jnp.int32, (1, LANES), 1)
    rows, columns = kept.shape

    def strip(i, sums):
        at = pl.ds(pl.multiple_of(i * 16, 16), 16)
        cross, mine, theirs = sums
        for c in range(columns // LANES):
            lanes = slice(c * LANES, (c + 1) * LANES)
            a = kept[at, lanes].astype(jnp.float32)
            b = received[at, lanes].astype(jnp.float32)
            cross, mine, theirs = cross + a * b, mine + a * a, theirs + b * b
        return cross, mine, theirs

    zero = jnp.zeros((16, LANES), jnp.float32)
    sums = lax.fori_loop(0, rows // 16, strip, (zero, zero, zero))
    result = before[...]
    for place, value in zip((0, 1 + first_at[0], 2 - first_at[0]), sums):
        total = jnp.sum(jnp.sum(value, axis=0, keepdims=True), axis=1, keepdims=True)
        result = result + jnp.where(lane == place, total, 0.0)
    out[...] = result


def partial_sums(bit, before, kept, received):
    return pl.pallas_call(
        partial_kernel,
        in_specs=[pl.BlockSpec(memory_space=pltpu.SMEM)] + [pl.BlockSpec(memory_space=pltpu.VMEM)] * 3,
        out_shape=jax.ShapeDtypeStruct((1, LANES), jnp.float32),
        scratch_shapes=[pltpu.VMEM((8, LANES), jnp.float32)],
        compiler_params=pltpu.CompilerParams(vmem_limit_bytes=VMEM_LIMIT),
        cost_estimate=SMALL,
        name="partial_sums",
    )(bit.reshape(1).astype(jnp.int32), before, kept, received)


def update_kernel(bit, sums, momentum, kept_0, kept_1, received_0, received_1, out):
    half = kept_0.shape[1]
    lower = bit[0] == 0
    lower_factor = 1.0 - sums[0, 0] / (2.0 * sums[0, 1])
    upper_factor = 1.0 - sums[0, 0] / (2.0 * sums[0, 2])
    factor = jnp.where(lower, lower_factor, upper_factor)
    other = jnp.where(lower, upper_factor, lower_factor)
    for at, a, b in ((slice(0, half), kept_0, received_0), (slice(half, 2 * half), kept_1, received_1)):
        out[:, at] = 0.9 * momentum[:, at] + (
            factor * a[...].astype(jnp.float32) + other * b[...].astype(jnp.float32)
        )


def update(bit, sums, momentum, kept, received):
    rows, columns = momentum.shape
    tile = math.gcd(rows, 128)
    spec = lambda width: pl.BlockSpec((tile, width), lambda i, *_: (i, 0))
    return pl.pallas_call(
        update_kernel,
        grid_spec=pltpu.PrefetchScalarGridSpec(
            num_scalar_prefetch=1,
            grid=(rows // tile,),
            in_specs=[pl.BlockSpec(sums.shape, lambda i, *_: (0, 0), memory_space=pltpu.SMEM), spec(columns)] + [spec(columns // 2)] * 4,
            out_specs=spec(columns),
        ),
        out_shape=jax.ShapeDtypeStruct(momentum.shape, jnp.float32),
        compiler_params=pltpu.CompilerParams(vmem_limit_bytes=VMEM_LIMIT),
        cost_estimate=SMALL,
        name="update",
    )(bit.reshape(1).astype(jnp.int32), sums, momentum, *kept, *received)


def body(inputs, weight, targets, momentum):
    groups = lax.axis_size("dp")
    parts = lax.axis_size("tensor")
    depth = groups.bit_length() - 1
    me = lax.axis_index("dp")
    part = lax.axis_index("tensor")
    rows, depth_width = inputs.shape
    columns = weight.shape[1]
    block = depth_width // groups
    width = depth_width // QUAD // parts
    per_block = block // width
    place = me % QUAD

    def columns_of(at, start, size):
        first = (QUAD * (start // block) + at) * block + start % block
        return lax.dynamic_slice(inputs, (0, first), (rows, size)).T

    slabs = [columns_of(place ^ k, part * width, width) for k in range(1, QUAD)]
    slabs, ready = lax.optimization_barrier((slabs, inputs))
    arrived = [exchange(s, "dp", k + 1) for k, s in enumerate(slabs)]

    def shared_far(piece):
        pieces, mask = [piece], parts // 2
        while mask > 1:
            pieces = pieces + [exchange(p, "tensor", mask) for p in pieces]
            mask //= 2
        return pieces

    def shared_near(pieces):
        return pieces + [exchange(p, "tensor", 1) for p in pieces]

    left = forward(ready, in_hbm(weight), targets, 0, 2)
    arrived[:2], left, ready = lax.optimization_barrier((arrived[:2], left, ready))
    y_left, z_left = exchange(left, "dp", 1), exchange(left, "dp", 2)
    right = forward(ready, in_hbm(weight), targets, 1, 2)
    y_right, z_right = exchange(right, "dp", 1), exchange(right, "dp", 2)
    near_inputs = shared_far(jnp.stack(arrived[:2]))
    sources = [part]
    mask = parts // 2
    while mask:
        sources = sources + [s ^ mask for s in sources]
        mask //= 2
    bit = me >> 2 & 1
    idx = jnp.stack([place, bit, part & 1] + sources).astype(jnp.int32)
    sums, own = own_gram(idx, in_hbm(inputs), left, right, width, block)
    left, right, y_left, z_left, own, near_inputs, arrived[2] = lax.optimization_barrier(
        (left, right, y_left, z_left, own, near_inputs, arrived[2])
    )
    near_inputs = shared_near(near_inputs)
    send, keep = input_grad_part(idx, parts, in_hbm(weight), left, right)
    send, keep, y_right, z_right, z_left, far_inputs = lax.optimization_barrier(
        (send, keep, y_right, z_right, z_left, arrived[2])
    )
    away = exchange(send, "tensor", 1)
    far_left, far_right = exchange(z_left, "dp", 1), exchange(y_right, "dp", 2)
    far_inputs = shared_far(far_inputs)

    def summed_terms(terms):
        total = sum(term.astype(jnp.float32) for term in terms)
        return total.astype(jnp.bfloat16)

    def halved(terms, mask):
        terms = [t.reshape(t.shape[0] // 2, 2, *t.shape[1:]) for t in terms]
        high = (part & mask) // mask
        sent = summed_terms([lax.dynamic_index_in_dim(t, 1 - high, 1, False) for t in terms])
        return sent, [lax.dynamic_index_in_dim(t, high, 1, False) for t in terms]

    send, terms = halved([keep, away], 2)
    send, sums = lax.optimization_barrier((send, sums))

    sums, grads = near_gram(idx, sums, own, near_inputs, (y_left, y_right, z_left, z_right))
    far_inputs, sums = lax.optimization_barrier((far_inputs, sums))
    far_inputs = shared_near(far_inputs)
    sums, last = far_gram(idx, sums, own, far_inputs, far_left, far_right, grads)
    sums = total_over(sums, 2)
    send, sums = lax.optimization_barrier((send, sums))
    terms.append(exchange(send, "tensor", 2))
    mask = 4
    while mask < parts:
        send, terms = halved(terms, mask)
        terms.append(exchange(send, "tensor", mask))
        mask *= 2
    summed = summed_terms(terms)[0]

    half = columns // 2

    def merged_half(flip, h):
        return merge(idx, flip, sums, own, grads, last, rows**-0.5, per_block, width, h, half)

    sent = [merged_half(True, h) for h in range(2)]
    received = [exchange(s, "dp", 4) for s in sent]
    _, sums = lax.optimization_barrier((sent, sums))
    kept = [merged_half(False, h) for h in range(2)]
    for level in range(2, depth):
        if level > 2:
            lower = bit == 0
            lower_factor = 1.0 - sums[0, 0] / (2.0 * sums[0, 1])
            upper_factor = 1.0 - sums[0, 0] / (2.0 * sums[0, 2])
            factor = jnp.where(lower, lower_factor, upper_factor)
            other = jnp.where(lower, upper_factor, lower_factor)
            merged = [
                factor * a.astype(jnp.float32) + other * b.astype(jnp.float32) for a, b in zip(kept, received)
            ]
            bit = me >> level & 1
            paired = [v.reshape(v.shape[0] // (2 * block), 2, block, v.shape[1]) for v in merged]
            kept = [jnp.where(bit == 0, v[:, 0], v[:, 1]).reshape(-1, v.shape[-1]) for v in paired]
            sent = [jnp.where(bit == 0, v[:, 1], v[:, 0]).reshape(-1, v.shape[-1]) for v in paired]
            received = [exchange(s.astype(jnp.bfloat16), "dp", 2**level) for s in sent]
        sums, summed = lax.optimization_barrier((jnp.zeros((1, LANES), jnp.float32), summed))
        for a, b in zip(kept, received):
            sums = partial_sums(bit, sums, a, b)
        sums = total_over(sums, level + 1)
    new_momentum = update(bit, sums, momentum, kept, received)
    return (summed, new_momentum, jnp.sqrt(sums[0, 1:3]) / depth_width)


def solution(mesh):
    return jax.shard_map(
        body,
        mesh=mesh,
        in_specs=(P("dp", None), P(None, "tensor"), P("dp", "tensor"), P("dp", "tensor")),
        out_specs=(P("tensor", "dp"), P("dp", "tensor"), P()),
        check_vma=False,
    )
```

```python
import functools
import math

import jax
import jax.numpy as jnp
from jax import lax
from jax.experimental import pallas as pl
from jax.experimental.pallas import tpu as pltpu
from jax.sharding import PartitionSpec as P

QUAD = 4
LANES = 128
SMALL = pl.CostEstimate(flops=1, bytes_accessed=1, transcendentals=0)
VMEM_LIMIT = 18 * 2**20
IN_PLACE_VMEM = 8 * 2**20
FULL_VMEM = 20 * 2**20


def in_hbm(value):
    return pltpu.with_memory_space_constraint(value, pltpu.HBM)


def exchange(value, axis, mask):
    pairs = [(source, source ^ mask) for source in range(lax.axis_size(axis))]
    return lax.ppermute(value, axis, pairs)


def total_over(value, dp_bits):
    hops = [("tensor", 1)] + [("dp", 2**bit) for bit in range(dp_bits)]
    mask = 2
    while mask < lax.axis_size("tensor"):
        hops.append(("tensor", mask))
        mask *= 2
    for axis, mask in hops:
        value = value + exchange(value, axis, mask)
    return value


def dot(a, b):
    return jnp.dot(a, b, preferred_element_type=jnp.float32)


def pair_sums(pairs, strips, rows, load, acc):
    def strip(i, sums):
        sums = list(sums)
        for tile in load(i * rows):
            for n, (a, b) in enumerate(pairs):
                sums[n] = sums[n] + tile[a] * tile[b]
        return tuple(sums)

    sums = lax.fori_loop(0, strips, strip, tuple(acc[n] for n in range(len(pairs))))
    for n in range(len(pairs)):
        acc[n] = sums[n]


def place_sums(place, pairs, acc, result):
    lane = lax.broadcasted_iota(jnp.int32, (1, LANES), 1)
    turn = place * (QUAD + 1)
    for n, (a, b) in enumerate(pairs):
        value = jnp.sum(jnp.sum(acc[n], axis=0, keepdims=True), axis=1, keepdims=True)
        first = jnp.bitwise_xor(QUAD * a + b, turn)
        second = jnp.bitwise_xor(QUAD * b + a, turn)
        result = jnp.where((lane == first) | (lane == second), value, result)
    return result


def lanes_of(columns):
    return [slice(c, c + LANES) for c in range(0, columns, LANES)]


NEAR_PAIRS = [(0, 1), (0, 2), (1, 1), (1, 2), (2, 2)]
FAR_PAIRS = [(a, QUAD - 1) for a in range(QUAD)]


def forward_kernel(x, w, targets, out):
    out[...] = (dot(x[...], w[...]) - targets[...].astype(jnp.float32)).astype(out.dtype)


def forward(inputs, weight, targets, part, parts):
    rows, inner = inputs.shape
    columns = weight.shape[1] // parts
    tile = math.gcd(columns, 256)
    first = part * columns // tile
    return pl.pallas_call(
        forward_kernel,
        grid=(columns // tile,),
        in_specs=[
            pl.BlockSpec((rows, inner), lambda j: (0, 0), pipeline_mode=pl.Buffered(1)),
            pl.BlockSpec((inner, tile), lambda j: (0, first + j)),
            pl.BlockSpec((rows, tile), lambda j: (0, first + j)),
        ],
        out_specs=pl.BlockSpec((rows, tile), lambda j: (0, j)),
        out_shape=jax.ShapeDtypeStruct((rows, columns), jnp.bfloat16),
        compiler_params=pltpu.CompilerParams(vmem_limit_bytes=FULL_VMEM),
        cost_estimate=SMALL,
        name="forward",
    )(inputs, weight, targets)


def input_grad_kernel(idx, w_send, w_keep, left, right, send, keep, turned):
    half = left.shape[1]

    @pl.when(pl.program_id(0) == 0)
    def _():
        turned[:half] = left[...].T
        turned[half:] = right[...].T

    for w, out in ((w_send, send), (w_keep, keep)):
        out[0] = dot(w[...], turned[...]).astype(out.dtype)


def input_grad_part(idx, parts, weight, left, right):
    inner, columns = weight.shape
    rows = left.shape[0]
    block = inner // parts
    tile = math.gcd(block, 512)
    per_block = block // tile

    def blocks_of(flip):
        def at(j, idx):
            parity = 1 - idx[PARITY] if flip else idx[PARITY]
            return ((2 * (j // per_block) + parity) * per_block + j % per_block, 0)

        return pl.BlockSpec((tile, columns), at)

    out = pltpu.HBM((parts // 2, block, rows), jnp.bfloat16)
    return pl.pallas_call(
        input_grad_kernel,
        grid_spec=pltpu.PrefetchScalarGridSpec(
            num_scalar_prefetch=1,
            grid=(parts // 2 * per_block,),
            in_specs=[blocks_of(True), blocks_of(False)] + [once(left.shape, (0, 0))] * 2,
            out_specs=[pl.BlockSpec((1, tile, rows), lambda j, idx: (j // per_block, j % per_block, 0))] * 2,
            scratch_shapes=[pltpu.VMEM((columns, rows), jnp.bfloat16)],
        ),
        out_shape=[out, out],
        compiler_params=pltpu.CompilerParams(vmem_limit_bytes=VMEM_LIMIT),
        cost_estimate=SMALL,
        name="input_grad_part",
    )(idx, weight, weight, left, right)


def fill(tile, xt, left, right):
    half = left.shape[1]
    tile[:, :half] = dot(xt, left[...])
    tile[:, half:] = dot(xt, right[...])


STRIP = 16


def strip_at(first):
    return pl.ds(pl.multiple_of(first, STRIP), STRIP)


def own_kernel(idx, x, left, right, out, grads, tile, acc):
    step = pl.program_id(0)
    half = left.shape[1]

    @pl.when(step == 0)
    def _():
        acc[...] = jnp.zeros_like(acc)

    for at, error in ((0, left), (half, right)):
        tile[:, at:at + half] = lax.dot_general(
            x[...], error[...], (((0,), (0,)), ((), ())), preferred_element_type=jnp.float32
        )

    def load(first):
        at = strip_at(first)
        for lanes in lanes_of(tile.shape[1]):
            mine = tile[at, lanes]
            grads[at, lanes] = mine.astype(grads.dtype)
            yield [mine]

    pair_sums([(0, 0)], tile.shape[0] // STRIP, STRIP, load, acc)

    @pl.when(step == pl.num_programs(0) - 1)
    def _():
        out[...] = place_sums(idx[PLACE], [(0, 0)], acc, jnp.zeros((1, LANES), jnp.float32))


def own_gram(idx, inputs, left, right, width, block):
    rows, inner = inputs.shape
    columns = 2 * left.shape[1]
    steps = inner // (QUAD * width)
    per_block = block // width

    def tile(j, idx):
        return (QUAD * (j // per_block) + idx[PLACE]) * per_block + j % per_block

    return pl.pallas_call(
        own_kernel,
        grid_spec=pltpu.PrefetchScalarGridSpec(
            num_scalar_prefetch=1,
            grid=(steps,),
            in_specs=[pl.BlockSpec((rows, width), lambda j, idx: (0, tile(j, idx)))]
            + [once(left.shape, (0, 0))] * 2,
            out_specs=[
                pl.BlockSpec((1, LANES), lambda j, idx: (0, 0)),
                pl.BlockSpec((width, columns), lambda j, idx: (j, 0)),
            ],
            scratch_shapes=[
                pltpu.VMEM((width, columns), jnp.float32),
                pltpu.VMEM((1, 16, LANES), jnp.float32),
            ],
        ),
        out_shape=[
            jax.ShapeDtypeStruct((1, LANES), jnp.float32),
            jax.ShapeDtypeStruct((steps * width, columns), jnp.bfloat16),
        ],
        compiler_params=pltpu.CompilerParams(vmem_limit_bytes=VMEM_LIMIT),
        cost_estimate=SMALL,
        name="own_gram",
    )(idx, inputs, left, right)


def near_kernel(pieces, idx, before, own, y_left, y_right, z_left, z_right, *refs):
    others, (out, grads, tiles, acc) = refs[:pieces], refs[pieces:]
    width = tiles.shape[1]
    acc[...] = jnp.zeros_like(acc)
    for q, other in enumerate(others):
        fill(tiles.at[0], other[0], y_left, y_right)
        fill(tiles.at[1], other[1], z_left, z_right)

        def load(first):
            at, there = strip_at(first), strip_at(idx[TILE + q] * width + first)
            for lanes in lanes_of(tiles.shape[2]):
                tile = [tiles[k, at, lanes] for k in range(QUAD - 2)]
                for k in range(QUAD - 2):
                    grads[k, there, lanes] = tile[k].astype(grads.dtype)
                yield [own[there, lanes].astype(jnp.float32)] + tile

        pair_sums(NEAR_PAIRS, width // STRIP, STRIP, load, acc)
    out[...] = place_sums(idx[PLACE], NEAR_PAIRS, acc, before[...])


def far_kernel(pieces, idx, before, left, right, own, grads, *refs):
    others, (out, last, tile, acc) = refs[:pieces], refs[pieces:]
    width = tile.shape[0]
    acc[...] = jnp.zeros_like(acc)
    for q, other in enumerate(others):
        fill(tile, other[...], left, right)

        def load(first):
            at, there = strip_at(first), strip_at(idx[TILE + q] * width + first)
            for lanes in lanes_of(tile.shape[1]):
                mine = tile[at, lanes]
                last[there, lanes] = mine.astype(last.dtype)
                three = [own[there, lanes]] + [grads[k, there, lanes] for k in range(QUAD - 2)]
                yield [v.astype(jnp.float32) for v in three] + [mine]

        pair_sums(FAR_PAIRS, width // STRIP, STRIP, load, acc)
    out[...] = place_sums(idx[PLACE], FAR_PAIRS, acc, before[...])


def once(shape, at):
    return pl.BlockSpec(shape, lambda j, idx: at, pipeline_mode=pl.Buffered(1))


PLACE, BIT, PARITY, TILE = 0, 1, 2, 3


def in_place(kernel, inputs, out_shape, scratch_shapes, name):
    return pl.pallas_call(
        kernel,
        in_specs=[pl.BlockSpec(memory_space=m) for m, _ in inputs],
        out_specs=[pl.BlockSpec(memory_space=pltpu.VMEM)] * len(out_shape),
        out_shape=out_shape,
        scratch_shapes=scratch_shapes,
        compiler_params=pltpu.CompilerParams(vmem_limit_bytes=IN_PLACE_VMEM),
        cost_estimate=SMALL,
        name=name,
    )(*[v for _, v in inputs])


def near_gram(idx, before, own, others, errors):
    width = others[0].shape[-2]
    rows, columns = own.shape
    return in_place(
        functools.partial(near_kernel, len(others)),
        [(pltpu.SMEM, idx)] + [(pltpu.VMEM, v) for v in (before, own, *errors, *others)],
        [
            jax.ShapeDtypeStruct((1, LANES), jnp.float32),
            jax.ShapeDtypeStruct((QUAD - 2, rows, columns), jnp.bfloat16),
        ],
        [
            pltpu.VMEM((QUAD - 2, width, columns), jnp.float32),
            pltpu.VMEM((len(NEAR_PAIRS), STRIP, LANES), jnp.float32),
        ],
        "near_gram",
    )


def far_gram(idx, before, own, others, left, right, grads):
    width = others[0].shape[-2]
    rows, columns = own.shape
    return in_place(
        functools.partial(far_kernel, len(others)),
        [(pltpu.SMEM, idx)] + [(pltpu.VMEM, v) for v in (before, left, right, own, grads, *others)],
        [
            jax.ShapeDtypeStruct((1, LANES), jnp.float32),
            jax.ShapeDtypeStruct((rows, columns), jnp.bfloat16),
        ],
        [
            pltpu.VMEM((width, columns), jnp.float32),
            pltpu.VMEM((len(FAR_PAIRS), STRIP, LANES), jnp.float32),
        ],
        "far_gram",
    )


def merge_factors(gram_at):
    factors = [None] * QUAD
    for a, b in ((0, 1), (2, 3)):
        cross = gram_at(a, b)
        factors[a] = 1.0 - cross / (2.0 * gram_at(a, a))
        factors[b] = 1.0 - cross / (2.0 * gram_at(b, b))

    def product(left, right):
        return sum(factors[a] * factors[b] * gram_at(a, b) for a in left for b in right)

    cross = product((0, 1), (2, 3))
    first = 1.0 - cross / (2.0 * product((0, 1), (0, 1)))
    second = 1.0 - cross / (2.0 * product((2, 3), (2, 3)))
    return [factors[0] * first, factors[1] * first, factors[2] * second, factors[3] * second]


def merge_kernel(scale, flip, per_block, width, at, idx, sums, own, grads, last, out):
    turn = idx[PLACE] * (QUAD + 1)
    factors = merge_factors(lambda a, b: sums[0, jnp.bitwise_xor(QUAD * a + b, turn)])
    factors = [factor * scale for factor in factors]
    bit = 1 - idx[BIT] if flip else idx[BIT]
    columns = out.shape[1]
    for j in range(out.shape[0] // width):
        tile = (2 * (j // per_block) + bit) * per_block + j % per_block

        def strip(i, carry):
            there, here = strip_at(tile * width + i * STRIP), strip_at(j * width + i * STRIP)
            for lanes in lanes_of(columns):
                from_lanes = slice(at * columns + lanes.start, at * columns + lanes.stop)
                four = (own[there, from_lanes], grads[0, there, from_lanes])
                four += (grads[1, there, from_lanes], last[there, from_lanes])
                total = factors[0] * four[0].astype(jnp.float32)
                for factor, value in zip(factors[1:], four[1:]):
                    total = total + factor * value.astype(jnp.float32)
                out[here, lanes] = total.astype(out.dtype)
            return carry

        lax.fori_loop(0, width // STRIP, strip, 0)


def merge(idx, flip, sums, own, grads, last, scale, per_block, width, at, columns):
    return in_place(
        functools.partial(merge_kernel, scale, flip, per_block, width, at),
        [(pltpu.SMEM, idx), (pltpu.SMEM, sums)] + [(pltpu.VMEM, v) for v in (own, grads, last)],
        [jax.ShapeDtypeStruct((own.shape[0] // 2, columns), jnp.bfloat16)],
        [],
        "merge",
    )[0]


def partial_kernel(first_at, before, kept, received, out, acc):
    lane = lax.broadcasted_iota(jnp.int32, (1, LANES), 1)
    rows, columns = kept.shape

    def strip(i, sums):
        at = pl.ds(pl.multiple_of(i * 16, 16), 16)
        cross, mine, theirs = sums
        for c in range(columns // LANES):
            lanes = slice(c * LANES, (c + 1) * LANES)
            a = kept[at, lanes].astype(jnp.float32)
            b = received[at, lanes].astype(jnp.float32)
            cross, mine, theirs = cross + a * b, mine + a * a, theirs + b * b
        return cross, mine, theirs

    zero = jnp.zeros((16, LANES), jnp.float32)
    sums = lax.fori_loop(0, rows // 16, strip, (zero, zero, zero))
    result = before[...]
    for place, value in zip((0, 1 + first_at[0], 2 - first_at[0]), sums):
        total = jnp.sum(jnp.sum(value, axis=0, keepdims=True), axis=1, keepdims=True)
        result = result + jnp.where(lane == place, total, 0.0)
    out[...] = result


def partial_sums(bit, before, kept, received):
    return pl.pallas_call(
        partial_kernel,
        in_specs=[pl.BlockSpec(memory_space=pltpu.SMEM)] + [pl.BlockSpec(memory_space=pltpu.VMEM)] * 3,
        out_shape=jax.ShapeDtypeStruct((1, LANES), jnp.float32),
        scratch_shapes=[pltpu.VMEM((8, LANES), jnp.float32)],
        compiler_params=pltpu.CompilerParams(vmem_limit_bytes=VMEM_LIMIT),
        cost_estimate=SMALL,
        name="partial_sums",
    )(bit.reshape(1).astype(jnp.int32), before, kept, received)


def update_kernel(norm, bit, sums, momentum, kept_0, kept_1, received_0, received_1, out, norms):
    half = kept_0.shape[1]
    lower = bit[0] == 0
    lower_factor = 1.0 - sums[0, 0] / (2.0 * sums[0, 1])
    upper_factor = 1.0 - sums[0, 0] / (2.0 * sums[0, 2])
    factor = jnp.where(lower, lower_factor, upper_factor)
    other = jnp.where(lower, upper_factor, lower_factor)

    def strip(i, carry):
        at = strip_at(i * STRIP)
        for left, a, b in ((0, kept_0, received_0), (half, kept_1, received_1)):
            for lanes in lanes_of(half):
                to = slice(left + lanes.start, left + lanes.stop)
                out[at, to] = 0.9 * momentum[at, to] + (
                    factor * a[at, lanes].astype(jnp.float32) + other * b[at, lanes].astype(jnp.float32)
                )
        return carry

    lax.fori_loop(0, out.shape[0] // STRIP, strip, 0)
    for n in range(2):
        norms[n] = jnp.sqrt(sums[0, 1 + n]) / norm


def update(bit, sums, momentum, kept, received, norm):
    vmem = pl.BlockSpec(memory_space=pltpu.VMEM)
    smem = pl.BlockSpec(memory_space=pltpu.SMEM)
    return pl.pallas_call(
        functools.partial(update_kernel, norm),
        in_specs=[smem, smem] + [vmem] * 5,
        out_specs=[vmem, smem],
        out_shape=[
            jax.ShapeDtypeStruct(momentum.shape, jnp.float32),
            jax.ShapeDtypeStruct((2,), jnp.float32),
        ],
        compiler_params=pltpu.CompilerParams(vmem_limit_bytes=VMEM_LIMIT),
        cost_estimate=SMALL,
        name="update",
    )(bit.reshape(1).astype(jnp.int32), sums, momentum, *kept, *received)


def body(inputs, weight, targets, momentum):
    groups = lax.axis_size("dp")
    parts = lax.axis_size("tensor")
    depth = groups.bit_length() - 1
    me = lax.axis_index("dp")
    part = lax.axis_index("tensor")
    rows, depth_width = inputs.shape
    columns = weight.shape[1]
    block = depth_width // groups
    width = depth_width // QUAD // parts
    per_block = block // width
    place = me % QUAD

    def columns_of(at, start, size):
        first = (QUAD * (start // block) + at) * block + start % block
        return lax.dynamic_slice(inputs, (0, first), (rows, size)).T

    slabs = [columns_of(place ^ k, part * width, width) for k in range(1, QUAD)]
    slabs, ready = lax.optimization_barrier((slabs, inputs))
    arrived = [exchange(s, "dp", k + 1) for k, s in enumerate(slabs)]

    def shared_far(piece):
        pieces, mask = [piece], parts // 2
        while mask > 1:
            pieces = pieces + [exchange(p, "tensor", mask) for p in pieces]
            mask //= 2
        return pieces

    def shared_near(pieces):
        return pieces + [exchange(p, "tensor", 1) for p in pieces]

    left = forward(ready, in_hbm(weight), targets, 0, 2)
    arrived[:2], left, ready = lax.optimization_barrier((arrived[:2], left, ready))
    y_left, z_left = exchange(left, "dp", 1), exchange(left, "dp", 2)
    right = forward(ready, in_hbm(weight), targets, 1, 2)
    y_right, z_right = exchange(right, "dp", 1), exchange(right, "dp", 2)
    near_inputs = shared_far(jnp.stack(arrived[:2]))
    sources = [part]
    mask = parts // 2
    while mask:
        sources = sources + [s ^ mask for s in sources]
        mask //= 2
    bit = me >> 2 & 1
    idx = jnp.stack([place, bit, part & 1] + sources).astype(jnp.int32)
    sums, own = own_gram(idx, in_hbm(inputs), left, right, width, block)
    left, right, y_left, z_left, own, near_inputs, arrived[2] = lax.optimization_barrier(
        (left, right, y_left, z_left, own, near_inputs, arrived[2])
    )
    near_inputs = shared_near(near_inputs)
    send, keep = input_grad_part(idx, parts, in_hbm(weight), left, right)
    send, keep, y_right, z_right, z_left, far_inputs = lax.optimization_barrier(
        (send, keep, y_right, z_right, z_left, arrived[2])
    )
    away = exchange(send, "tensor", 1)
    far_left, far_right = exchange(z_left, "dp", 1), exchange(y_right, "dp", 2)
    far_inputs = shared_far(far_inputs)

    def summed_terms(terms):
        total = sum(term.astype(jnp.float32) for term in terms)
        return total.astype(jnp.bfloat16)

    def halved(terms, mask):
        terms = [t.reshape(t.shape[0] // 2, 2, *t.shape[1:]) for t in terms]
        high = (part & mask) // mask
        sent = summed_terms([lax.dynamic_index_in_dim(t, 1 - high, 1, False) for t in terms])
        return sent, [lax.dynamic_index_in_dim(t, high, 1, False) for t in terms]

    send, terms = halved([keep, away], 2)
    send, sums = lax.optimization_barrier((send, sums))

    sums, grads = near_gram(idx, sums, own, near_inputs, (y_left, y_right, z_left, z_right))
    far_inputs, sums = lax.optimization_barrier((far_inputs, sums))
    far_inputs = shared_near(far_inputs)
    sums, last = far_gram(idx, sums, own, far_inputs, far_left, far_right, grads)
    sums = total_over(sums, 2)
    half = columns // 2

    def merged_half(flip, h):
        return merge(idx, flip, sums, own, grads, last, rows**-0.5, per_block, width, h, half)

    sent = [merged_half(True, h) for h in range(2)]
    received = [exchange(s, "dp", 4) for s in sent]
    send, _ = lax.optimization_barrier((send, sent[0]))
    terms.append(exchange(send, "tensor", 2))
    mask = 4
    while mask < parts:
        send, terms = halved(terms, mask)
        terms.append(exchange(send, "tensor", mask))
        mask *= 2
    summed = summed_terms(terms)[0]
    _, sums = lax.optimization_barrier((sent, sums))
    kept = [merged_half(False, h) for h in range(2)]
    for level in range(2, depth):
        if level > 2:
            lower = bit == 0
            lower_factor = 1.0 - sums[0, 0] / (2.0 * sums[0, 1])
            upper_factor = 1.0 - sums[0, 0] / (2.0 * sums[0, 2])
            factor = jnp.where(lower, lower_factor, upper_factor)
            other = jnp.where(lower, upper_factor, lower_factor)
            merged = [
                factor * a.astype(jnp.float32) + other * b.astype(jnp.float32) for a, b in zip(kept, received)
            ]
            bit = me >> level & 1
            paired = [v.reshape(v.shape[0] // (2 * block), 2, block, v.shape[1]) for v in merged]
            kept = [jnp.where(bit == 0, v[:, 0], v[:, 1]).reshape(-1, v.shape[-1]) for v in paired]
            sent = [jnp.where(bit == 0, v[:, 1], v[:, 0]).reshape(-1, v.shape[-1]) for v in paired]
            received = [exchange(s.astype(jnp.bfloat16), "dp", 2**level) for s in sent]
        sums, summed = lax.optimization_barrier((jnp.zeros((1, LANES), jnp.float32), summed))
        for a, b in zip(kept, received):
            sums = partial_sums(bit, sums, a, b)
        sums = total_over(sums, level + 1)
    new_momentum, tree_norms = update(bit, sums, momentum, kept, received, depth_width)
    return (summed, new_momentum, tree_norms)


def solution(mesh):
    return jax.shard_map(
        body,
        mesh=mesh,
        in_specs=(P("dp", None), P(None, "tensor"), P("dp", "tensor"), P("dp", "tensor")),
        out_specs=(P("tensor", "dp"), P("dp", "tensor"), P()),
        check_vma=False,
    )
```

```python
import functools
import math

import jax
import jax.numpy as jnp
from jax import lax
from jax.experimental import pallas as pl
from jax.experimental.pallas import tpu as pltpu
from jax.sharding import PartitionSpec as P

QUAD = 4
LANES = 128
SMALL = pl.CostEstimate(flops=1, bytes_accessed=1, transcendentals=0)
VMEM_LIMIT = 18 * 2**20
IN_PLACE_VMEM = 8 * 2**20
FULL_VMEM = 20 * 2**20


def in_hbm(value):
    return pltpu.with_memory_space_constraint(value, pltpu.HBM)


def exchange(value, axis, mask):
    pairs = [(source, source ^ mask) for source in range(lax.axis_size(axis))]
    return lax.ppermute(value, axis, pairs)


def total_over(value, dp_bits):
    hops = [("tensor", 1)] + [("dp", 2**bit) for bit in range(dp_bits)]
    mask = 2
    while mask < lax.axis_size("tensor"):
        hops.append(("tensor", mask))
        mask *= 2
    for axis, mask in hops:
        value = value + exchange(value, axis, mask)
    return value


def dot(a, b):
    return jnp.dot(a, b, preferred_element_type=jnp.float32)


def pair_sums(pairs, strips, rows, load, acc):
    def strip(i, sums):
        sums = list(sums)
        for tile in load(i * rows):
            for n, (a, b) in enumerate(pairs):
                sums[n] = sums[n] + tile[a] * tile[b]
        return tuple(sums)

    sums = lax.fori_loop(0, strips, strip, tuple(acc[n] for n in range(len(pairs))))
    for n in range(len(pairs)):
        acc[n] = sums[n]


def place_sums(place, pairs, acc, result):
    lane = lax.broadcasted_iota(jnp.int32, (1, LANES), 1)
    turn = place * (QUAD + 1)
    for n, (a, b) in enumerate(pairs):
        value = jnp.sum(jnp.sum(acc[n], axis=0, keepdims=True), axis=1, keepdims=True)
        first = jnp.bitwise_xor(QUAD * a + b, turn)
        second = jnp.bitwise_xor(QUAD * b + a, turn)
        result = jnp.where((lane == first) | (lane == second), value, result)
    return result


def lanes_of(columns):
    return [slice(c, c + LANES) for c in range(0, columns, LANES)]


NEAR_PAIRS = [(0, 1), (0, 2), (1, 1), (1, 2), (2, 2)]
FAR_PAIRS = [(a, QUAD - 1) for a in range(QUAD)]


def forward_kernel(x, w, targets, out):
    out[...] = (dot(x[...], w[...]) - targets[...].astype(jnp.float32)).astype(out.dtype)


def forward(inputs, weight, targets, part, parts):
    rows, inner = inputs.shape
    columns = weight.shape[1] // parts
    tile = math.gcd(columns, 256)
    first = part * columns // tile
    return pl.pallas_call(
        forward_kernel,
        grid=(columns // tile,),
        in_specs=[
            pl.BlockSpec((rows, inner), lambda j: (0, 0), pipeline_mode=pl.Buffered(1)),
            pl.BlockSpec((inner, tile), lambda j: (0, first + j)),
            pl.BlockSpec((rows, tile), lambda j: (0, first + j)),
        ],
        out_specs=pl.BlockSpec((rows, tile), lambda j: (0, j)),
        out_shape=jax.ShapeDtypeStruct((rows, columns), jnp.bfloat16),
        compiler_params=pltpu.CompilerParams(vmem_limit_bytes=FULL_VMEM),
        cost_estimate=SMALL,
        name="forward",
    )(inputs, weight, targets)


def input_grad_kernel(idx, w_send, w_keep, left, right, send, keep, turned):
    half = left.shape[1]

    @pl.when(pl.program_id(0) == 0)
    def _():
        turned[:half] = left[...].T
        turned[half:] = right[...].T

    for w, out in ((w_send, send), (w_keep, keep)):
        out[0] = dot(w[...], turned[...]).astype(out.dtype)


def input_grad_part(idx, parts, weight, left, right):
    inner, columns = weight.shape
    rows = left.shape[0]
    block = inner // parts
    tile = math.gcd(block, 512)
    per_block = block // tile

    def blocks_of(flip):
        def at(j, idx):
            parity = 1 - idx[PARITY] if flip else idx[PARITY]
            return ((2 * (j // per_block) + parity) * per_block + j % per_block, 0)

        return pl.BlockSpec((tile, columns), at)

    out = pltpu.HBM((parts // 2, block, rows), jnp.bfloat16)
    return pl.pallas_call(
        input_grad_kernel,
        grid_spec=pltpu.PrefetchScalarGridSpec(
            num_scalar_prefetch=1,
            grid=(parts // 2 * per_block,),
            in_specs=[blocks_of(True), blocks_of(False)] + [once(left.shape, (0, 0))] * 2,
            out_specs=[pl.BlockSpec((1, tile, rows), lambda j, idx: (j // per_block, j % per_block, 0))] * 2,
            scratch_shapes=[pltpu.VMEM((columns, rows), jnp.bfloat16)],
        ),
        out_shape=[out, out],
        compiler_params=pltpu.CompilerParams(vmem_limit_bytes=VMEM_LIMIT),
        cost_estimate=SMALL,
        name="input_grad_part",
    )(idx, weight, weight, left, right)


def fill(tile, xt, left, right):
    half = left.shape[1]
    tile[:, :half] = dot(xt, left[...])
    tile[:, half:] = dot(xt, right[...])


STRIP = 16


def strip_at(first):
    return pl.ds(pl.multiple_of(first, STRIP), STRIP)


def own_kernel(idx, x, left, right, out, grads, tile, acc):
    step = pl.program_id(0)
    half = left.shape[1]

    @pl.when(step == 0)
    def _():
        acc[...] = jnp.zeros_like(acc)

    for at, error in ((0, left), (half, right)):
        tile[:, at:at + half] = lax.dot_general(
            x[...], error[...], (((0,), (0,)), ((), ())), preferred_element_type=jnp.float32
        )

    def load(first):
        at = strip_at(first)
        for lanes in lanes_of(tile.shape[1]):
            mine = tile[at, lanes]
            grads[at, lanes] = mine.astype(grads.dtype)
            yield [mine]

    pair_sums([(0, 0)], tile.shape[0] // STRIP, STRIP, load, acc)

    @pl.when(step == pl.num_programs(0) - 1)
    def _():
        out[...] = place_sums(idx[PLACE], [(0, 0)], acc, jnp.zeros((1, LANES), jnp.float32))


def own_gram(idx, inputs, left, right, width, block):
    rows, inner = inputs.shape
    columns = 2 * left.shape[1]
    steps = inner // (QUAD * width)
    per_block = block // width

    def tile(j, idx):
        return (QUAD * (j // per_block) + idx[PLACE]) * per_block + j % per_block

    return pl.pallas_call(
        own_kernel,
        grid_spec=pltpu.PrefetchScalarGridSpec(
            num_scalar_prefetch=1,
            grid=(steps,),
            in_specs=[pl.BlockSpec((rows, width), lambda j, idx: (0, tile(j, idx)))]
            + [once(left.shape, (0, 0))] * 2,
            out_specs=[
                pl.BlockSpec((1, LANES), lambda j, idx: (0, 0)),
                pl.BlockSpec((width, columns), lambda j, idx: (j, 0)),
            ],
            scratch_shapes=[
                pltpu.VMEM((width, columns), jnp.float32),
                pltpu.VMEM((1, 16, LANES), jnp.float32),
            ],
        ),
        out_shape=[
            jax.ShapeDtypeStruct((1, LANES), jnp.float32),
            jax.ShapeDtypeStruct((steps * width, columns), jnp.bfloat16),
        ],
        compiler_params=pltpu.CompilerParams(vmem_limit_bytes=VMEM_LIMIT),
        cost_estimate=SMALL,
        name="own_gram",
    )(idx, inputs, left, right)


def near_kernel(pieces, idx, before, own, y_left, y_right, z_left, z_right, *refs):
    others, (out, grads, tiles, acc) = refs[:pieces], refs[pieces:]
    width = tiles.shape[1]
    acc[...] = jnp.zeros_like(acc)
    for q, other in enumerate(others):
        fill(tiles.at[0], other[0], y_left, y_right)
        fill(tiles.at[1], other[1], z_left, z_right)

        def load(first):
            at, there = strip_at(first), strip_at(idx[TILE + q] * width + first)
            for lanes in lanes_of(tiles.shape[2]):
                tile = [tiles[k, at, lanes] for k in range(QUAD - 2)]
                for k in range(QUAD - 2):
                    grads[k, there, lanes] = tile[k].astype(grads.dtype)
                yield [own[there, lanes].astype(jnp.float32)] + tile

        pair_sums(NEAR_PAIRS, width // STRIP, STRIP, load, acc)
    out[...] = place_sums(idx[PLACE], NEAR_PAIRS, acc, before[...])


def far_kernel(pieces, idx, before, left, right, own, grads, *refs):
    others, (out, last, tile, acc) = refs[:pieces], refs[pieces:]
    width = tile.shape[0]
    acc[...] = jnp.zeros_like(acc)
    for q, other in enumerate(others):
        fill(tile, other[...], left, right)

        def load(first):
            at, there = strip_at(first), strip_at(idx[TILE + q] * width + first)
            for lanes in lanes_of(tile.shape[1]):
                mine = tile[at, lanes]
                last[there, lanes] = mine.astype(last.dtype)
                three = [own[there, lanes]] + [grads[k, there, lanes] for k in range(QUAD - 2)]
                yield [v.astype(jnp.float32) for v in three] + [mine]

        pair_sums(FAR_PAIRS, width // STRIP, STRIP, load, acc)
    out[...] = place_sums(idx[PLACE], FAR_PAIRS, acc, before[...])


def once(shape, at):
    return pl.BlockSpec(shape, lambda j, idx: at, pipeline_mode=pl.Buffered(1))


PLACE, BIT, PARITY, TILE = 0, 1, 2, 3


def in_place(kernel, inputs, out_shape, scratch_shapes, name):
    return pl.pallas_call(
        kernel,
        in_specs=[pl.BlockSpec(memory_space=m) for m, _ in inputs],
        out_specs=[pl.BlockSpec(memory_space=pltpu.VMEM)] * len(out_shape),
        out_shape=out_shape,
        scratch_shapes=scratch_shapes,
        compiler_params=pltpu.CompilerParams(vmem_limit_bytes=IN_PLACE_VMEM),
        cost_estimate=SMALL,
        name=name,
    )(*[v for _, v in inputs])


def near_gram(idx, before, own, others, errors):
    width = others[0].shape[-2]
    rows, columns = own.shape
    return in_place(
        functools.partial(near_kernel, len(others)),
        [(pltpu.SMEM, idx)] + [(pltpu.VMEM, v) for v in (before, own, *errors, *others)],
        [
            jax.ShapeDtypeStruct((1, LANES), jnp.float32),
            jax.ShapeDtypeStruct((QUAD - 2, rows, columns), jnp.bfloat16),
        ],
        [
            pltpu.VMEM((QUAD - 2, width, columns), jnp.float32),
            pltpu.VMEM((len(NEAR_PAIRS), STRIP, LANES), jnp.float32),
        ],
        "near_gram",
    )


def far_gram(idx, before, own, others, left, right, grads):
    width = others[0].shape[-2]
    rows, columns = own.shape
    return in_place(
        functools.partial(far_kernel, len(others)),
        [(pltpu.SMEM, idx)] + [(pltpu.VMEM, v) for v in (before, left, right, own, grads, *others)],
        [
            jax.ShapeDtypeStruct((1, LANES), jnp.float32),
            jax.ShapeDtypeStruct((rows, columns), jnp.bfloat16),
        ],
        [
            pltpu.VMEM((width, columns), jnp.float32),
            pltpu.VMEM((len(FAR_PAIRS), STRIP, LANES), jnp.float32),
        ],
        "far_gram",
    )


def merge_factors(gram_at):
    factors = [None] * QUAD
    for a, b in ((0, 1), (2, 3)):
        cross = gram_at(a, b)
        factors[a] = 1.0 - cross / (2.0 * gram_at(a, a))
        factors[b] = 1.0 - cross / (2.0 * gram_at(b, b))

    def product(left, right):
        return sum(factors[a] * factors[b] * gram_at(a, b) for a in left for b in right)

    cross = product((0, 1), (2, 3))
    first = 1.0 - cross / (2.0 * product((0, 1), (0, 1)))
    second = 1.0 - cross / (2.0 * product((2, 3), (2, 3)))
    return [factors[0] * first, factors[1] * first, factors[2] * second, factors[3] * second]


def merge_kernel(scale, flip, per_block, width, at, idx, sums, own, grads, last, out, tiles, sems):
    turn = idx[PLACE] * (QUAD + 1)
    bit = 1 - idx[BIT] if flip else idx[BIT]
    columns = out.shape[1]
    steps = out.shape[0] // width
    from_columns = pl.ds(at * columns, columns)
    copies = []
    for j in range(steps):
        tile = (2 * (j // per_block) + bit) * per_block + j % per_block
        there, here = pl.ds(pl.multiple_of(tile * width, width), width), pl.ds(j * width, width)
        sources = (own, grads.at[0], grads.at[1], last)
        for k, source in enumerate(sources):
            copy = pltpu.make_async_copy(source.at[there, from_columns], tiles.at[k, here], sems.at[j, k])
            copy.start()
            copies.append(copy)
    factors = merge_factors(lambda a, b: sums[0, jnp.bitwise_xor(QUAD * a + b, turn)])
    factors = [factor * scale for factor in factors]
    for copy in copies:
        copy.wait()

    def strip(i, carry):
        rows = strip_at(i * STRIP)
        for lanes in lanes_of(columns):
            total = factors[0] * tiles[0, rows, lanes].astype(jnp.float32)
            for k in range(1, QUAD):
                total = total + factors[k] * tiles[k, rows, lanes].astype(jnp.float32)
            out[rows, lanes] = total.astype(out.dtype)
        return carry

    lax.fori_loop(0, out.shape[0] // STRIP, strip, 0)


def merge(idx, flip, sums, own, grads, last, scale, per_block, width, at, columns):
    rows = own.shape[0] // 2
    return in_place(
        functools.partial(merge_kernel, scale, flip, per_block, width, at),
        [(pltpu.SMEM, idx), (pltpu.SMEM, sums)] + [(pltpu.HBM, in_hbm(v)) for v in (own, grads, last)],
        [jax.ShapeDtypeStruct((rows, columns), jnp.bfloat16)],
        [
            pltpu.VMEM((QUAD, rows, columns), jnp.bfloat16),
            pltpu.SemaphoreType.DMA((rows // width, QUAD)),
        ],
        "merge",
    )[0]


def partial_kernel(first_at, before, kept, received, out, acc):
    lane = lax.broadcasted_iota(jnp.int32, (1, LANES), 1)
    rows, columns = kept.shape

    def strip(i, sums):
        at = pl.ds(pl.multiple_of(i * 16, 16), 16)
        cross, mine, theirs = sums
        for c in range(columns // LANES):
            lanes = slice(c * LANES, (c + 1) * LANES)
            a = kept[at, lanes].astype(jnp.float32)
            b = received[at, lanes].astype(jnp.float32)
            cross, mine, theirs = cross + a * b, mine + a * a, theirs + b * b
        return cross, mine, theirs

    zero = jnp.zeros((16, LANES), jnp.float32)
    sums = lax.fori_loop(0, rows // 16, strip, (zero, zero, zero))
    result = before[...]
    for place, value in zip((0, 1 + first_at[0], 2 - first_at[0]), sums):
        total = jnp.sum(jnp.sum(value, axis=0, keepdims=True), axis=1, keepdims=True)
        result = result + jnp.where(lane == place, total, 0.0)
    out[...] = result


def partial_sums(bit, before, kept, received):
    return pl.pallas_call(
        partial_kernel,
        in_specs=[pl.BlockSpec(memory_space=pltpu.SMEM)] + [pl.BlockSpec(memory_space=pltpu.VMEM)] * 3,
        out_shape=jax.ShapeDtypeStruct((1, LANES), jnp.float32),
        scratch_shapes=[pltpu.VMEM((8, LANES), jnp.float32)],
        compiler_params=pltpu.CompilerParams(vmem_limit_bytes=VMEM_LIMIT),
        cost_estimate=SMALL,
        name="partial_sums",
    )(bit.reshape(1).astype(jnp.int32), before, kept, received)


def update_kernel(norm, bit, sums, momentum, kept_0, kept_1, received_0, received_1, out, norms):
    half = kept_0.shape[1]
    lower = bit[0] == 0
    lower_factor = 1.0 - sums[0, 0] / (2.0 * sums[0, 1])
    upper_factor = 1.0 - sums[0, 0] / (2.0 * sums[0, 2])
    factor = jnp.where(lower, lower_factor, upper_factor)
    other = jnp.where(lower, upper_factor, lower_factor)

    def strip(i, carry):
        at = strip_at(i * STRIP)
        for left, a, b in ((0, kept_0, received_0), (half, kept_1, received_1)):
            for lanes in lanes_of(half):
                to = slice(left + lanes.start, left + lanes.stop)
                out[at, to] = 0.9 * momentum[at, to] + (
                    factor * a[at, lanes].astype(jnp.float32) + other * b[at, lanes].astype(jnp.float32)
                )
        return carry

    lax.fori_loop(0, out.shape[0] // STRIP, strip, 0)
    for n in range(2):
        norms[n] = jnp.sqrt(sums[0, 1 + n]) / norm


def update(bit, sums, momentum, kept, received, norm):
    vmem = pl.BlockSpec(memory_space=pltpu.VMEM)
    smem = pl.BlockSpec(memory_space=pltpu.SMEM)
    return pl.pallas_call(
        functools.partial(update_kernel, norm),
        in_specs=[smem, smem] + [vmem] * 5,
        out_specs=[vmem, smem],
        out_shape=[
            jax.ShapeDtypeStruct(momentum.shape, jnp.float32),
            jax.ShapeDtypeStruct((2,), jnp.float32),
        ],
        compiler_params=pltpu.CompilerParams(vmem_limit_bytes=VMEM_LIMIT),
        cost_estimate=SMALL,
        name="update",
    )(bit.reshape(1).astype(jnp.int32), sums, momentum, *kept, *received)


def body(inputs, weight, targets, momentum):
    groups = lax.axis_size("dp")
    parts = lax.axis_size("tensor")
    depth = groups.bit_length() - 1
    me = lax.axis_index("dp")
    part = lax.axis_index("tensor")
    rows, depth_width = inputs.shape
    columns = weight.shape[1]
    block = depth_width // groups
    width = depth_width // QUAD // parts
    per_block = block // width
    place = me % QUAD

    def columns_of(at, start, size):
        first = (QUAD * (start // block) + at) * block + start % block
        return lax.dynamic_slice(inputs, (0, first), (rows, size)).T

    slabs = [columns_of(place ^ k, part * width, width) for k in range(1, QUAD)]
    slabs, ready = lax.optimization_barrier((slabs, inputs))
    arrived = [exchange(s, "dp", k + 1) for k, s in enumerate(slabs)]

    def shared_far(piece):
        pieces, mask = [piece], parts // 2
        while mask > 1:
            pieces = pieces + [exchange(p, "tensor", mask) for p in pieces]
            mask //= 2
        return pieces

    def shared_near(pieces):
        return pieces + [exchange(p, "tensor", 1) for p in pieces]

    left = forward(ready, in_hbm(weight), targets, 0, 2)
    arrived[:2], left, ready = lax.optimization_barrier((arrived[:2], left, ready))
    y_left, z_left = exchange(left, "dp", 1), exchange(left, "dp", 2)
    right = forward(ready, in_hbm(weight), targets, 1, 2)
    y_right, z_right = exchange(right, "dp", 1), exchange(right, "dp", 2)
    near_inputs = shared_far(jnp.stack(arrived[:2]))
    sources = [part]
    mask = parts // 2
    while mask:
        sources = sources + [s ^ mask for s in sources]
        mask //= 2
    bit = me >> 2 & 1
    idx = jnp.stack([place, bit, part & 1] + sources).astype(jnp.int32)
    sums, own = own_gram(idx, in_hbm(inputs), left, right, width, block)
    left, right, y_left, z_left, own, near_inputs, arrived[2] = lax.optimization_barrier(
        (left, right, y_left, z_left, own, near_inputs, arrived[2])
    )
    near_inputs = shared_near(near_inputs)
    send, keep = input_grad_part(idx, parts, in_hbm(weight), left, right)
    send, keep, y_right, z_right, z_left, far_inputs = lax.optimization_barrier(
        (send, keep, y_right, z_right, z_left, arrived[2])
    )
    away = exchange(send, "tensor", 1)
    far_left, far_right = exchange(z_left, "dp", 1), exchange(y_right, "dp", 2)
    far_inputs = shared_far(far_inputs)

    def summed_terms(terms):
        total = sum(term.astype(jnp.float32) for term in terms)
        return total.astype(jnp.bfloat16)

    def halved(terms, mask):
        terms = [t.reshape(t.shape[0] // 2, 2, *t.shape[1:]) for t in terms]
        high = (part & mask) // mask
        sent = summed_terms([lax.dynamic_index_in_dim(t, 1 - high, 1, False) for t in terms])
        return sent, [lax.dynamic_index_in_dim(t, high, 1, False) for t in terms]

    send, terms = halved([keep, away], 2)
    send, sums = lax.optimization_barrier((send, sums))

    sums, grads = near_gram(idx, sums, own, near_inputs, (y_left, y_right, z_left, z_right))
    far_inputs, sums = lax.optimization_barrier((far_inputs, sums))
    far_inputs = shared_near(far_inputs)
    sums, last = far_gram(idx, sums, own, far_inputs, far_left, far_right, grads)
    sums = total_over(sums, 2)
    half = columns // 2

    def merged_half(flip, h):
        return merge(idx, flip, sums, own, grads, last, rows**-0.5, per_block, width, h, half)

    sent = [merged_half(True, h) for h in range(2)]
    received = [exchange(s, "dp", 4) for s in sent]
    send, _ = lax.optimization_barrier((send, sent[0]))
    terms.append(exchange(send, "tensor", 2))
    mask = 4
    while mask < parts:
        send, terms = halved(terms, mask)
        terms.append(exchange(send, "tensor", mask))
        mask *= 2
    summed = summed_terms(terms)[0]
    _, sums = lax.optimization_barrier((sent, sums))
    kept = [merged_half(False, h) for h in range(2)]
    for level in range(2, depth):
        if level > 2:
            lower = bit == 0
            lower_factor = 1.0 - sums[0, 0] / (2.0 * sums[0, 1])
            upper_factor = 1.0 - sums[0, 0] / (2.0 * sums[0, 2])
            factor = jnp.where(lower, lower_factor, upper_factor)
            other = jnp.where(lower, upper_factor, lower_factor)
            merged = [
                factor * a.astype(jnp.float32) + other * b.astype(jnp.float32) for a, b in zip(kept, received)
            ]
            bit = me >> level & 1
            paired = [v.reshape(v.shape[0] // (2 * block), 2, block, v.shape[1]) for v in merged]
            kept = [jnp.where(bit == 0, v[:, 0], v[:, 1]).reshape(-1, v.shape[-1]) for v in paired]
            sent = [jnp.where(bit == 0, v[:, 1], v[:, 0]).reshape(-1, v.shape[-1]) for v in paired]
            received = [exchange(s.astype(jnp.bfloat16), "dp", 2**level) for s in sent]
        sums, summed = lax.optimization_barrier((jnp.zeros((1, LANES), jnp.float32), summed))
        for a, b in zip(kept, received):
            sums = partial_sums(bit, sums, a, b)
        sums = total_over(sums, level + 1)
    new_momentum, tree_norms = update(bit, sums, momentum, kept, received, depth_width)
    return (summed, new_momentum, tree_norms)


def solution(mesh):
    return jax.shard_map(
        body,
        mesh=mesh,
        in_specs=(P("dp", None), P(None, "tensor"), P("dp", "tensor"), P("dp", "tensor")),
        out_specs=(P("tensor", "dp"), P("dp", "tensor"), P()),
        check_vma=False,
    )
```
